1024 devices in a mesh: dp: 32 (over x, y_hi, core), tensor: 32 (over z, y_lo).
Axes of the slice: x: 4, y: 8 (y_hi: 4, y_lo: 2; y = y_hi * 2 + y_lo), z: 16, core: 2. Of those that a mesh axis runs over, the one named last changes fastest.
Arguments:
- latent_with_rope: bfloat16 [16384, 576], P('dp'), may hold values from -120 to 120
- latent_norm_weight: float32 [512], replicated, may hold values from 0.1 to 1.9
- expand_weight: bfloat16 [512, 32768], P(None, 'tensor'), may hold values from -0.25 to 0.25
- queries: bfloat16 [16384, 24576], P('dp', 'tensor'), may hold values from -64 to 64
- grad_output: bfloat16 [16384, 16384], P('dp', 'tensor'), may hold values from -24 to 24
Outputs:
- grad_queries: bfloat16 [16384, 24576], P('dp', 'tensor')
- grad_joint_latent: bfloat16 [16384, 576], P('dp')
- grad_up_weight: float32 [512, 32768], P('dp', 'tensor')
- grad_gain: float32 [512], replicated
The draws below stay inside these ranges and needn't reach their ends.
All inputs are finite; a program needn't handle non-finite values.
Results may differ from the reference program's by a relative error of at most 0.034.
Values may be sent and summed in bfloat16 or wider, within the bound.
A program may use at most 32 MiB of HBM per device.

```python
import math
import jax
import jax.numpy as jnp
from jax import lax

KEY_VALUE_RANK = 512
ROPE = 64
PLAIN_HEAD_DIM = 128
VALUE_HEAD_DIM = 128
HEAD_COUNT = 128
SEQ = 512
TOKEN_COUNT = 16384


def rope_values(key):
    folded = jax.random.fold_in(key, 11)
    first_key = jax.random.fold_in(folded, 0)
    gauss = jnp.clip(jax.random.normal(first_key, (TOKEN_COUNT, ROPE), jnp.float32), -4.0, 4.0)
    return gauss


def draw_latent_with_rope(key, part):
    rope = rope_values(key)
    key = jax.random.fold_in(key, 3)
    value_seed, row_key, column_seed = jax.random.split(key, 3)
    entry_items = jnp.clip(jax.random.normal(value_seed, (TOKEN_COUNT, KEY_VALUE_RANK), jnp.float32), -4.0, 4.0)
    row_scale = jnp.exp(jax.random.uniform(row_key, (TOKEN_COUNT, 1), jnp.float32, 0.0, math.log(10.0)))
    column_factor = jnp.exp(jax.random.uniform(column_seed, (1, KEY_VALUE_RANK), jnp.float32, math.log(0.3), math.log(3.0)))
    latent_state = entry_items * row_scale * column_factor
    return jnp.concatenate([latent_state, rope], axis=1).astype(jnp.bfloat16)


def draw_queries(key, part):
    key = jax.random.fold_in(key, 5)
    values = 0.5 * jnp.clip(jax.random.normal(key, (TOKEN_COUNT, HEAD_COUNT, PLAIN_HEAD_DIM + ROPE), jnp.float32), -6.0, 6.0)
    return values.reshape(TOKEN_COUNT, HEAD_COUNT * (PLAIN_HEAD_DIM + ROPE)).astype(jnp.bfloat16)


def block_scale(own_key, extent, cuts, least, high):
    level, own = 1.0, jax.random.fold_in(own_key, 6)
    for axis_at, shards_of in cuts:
        heights = jnp.exp(jax.random.uniform(jax.random.fold_in(own, axis_at), (shards_of,), jnp.float32, least / len(cuts), high / len(cuts)))
        level = level * jnp.repeat(heights, extent[axis_at] // shards_of).reshape([-1 if axis == axis_at else 1 for axis in range(len(extent))])
    return level


def noise(rng, dims, deviation, most, cuts=(), kind=jnp.bfloat16):
    result = jax.random.normal(rng, dims, jnp.float32) * deviation
    if len(cuts) > 0:
        result = block_scale(rng, dims, cuts, -0.22, 0.18) * result
    return jnp.clip(result, min=-most, max=most).astype(kind)


def setup_inputs(seed: int = 0) -> dict:
    streams_of = jax.random.split(jax.random.key(seed), 6)
    return {
        "latent_with_rope": draw_latent_with_rope(jax.random.fold_in(streams_of[5], 71), 0),
        "latent_norm_weight": jnp.clip(1.0 + 0.18 * jax.random.normal(streams_of[1], (KEY_VALUE_RANK,), jnp.float32), 0.1, 1.9),
        "expand_weight": noise(streams_of[2], (KEY_VALUE_RANK, HEAD_COUNT * (PLAIN_HEAD_DIM + VALUE_HEAD_DIM)), KEY_VALUE_RANK ** -0.5, 0.25, ((1, 32),)),
        "queries": draw_queries(jax.random.fold_in(streams_of[5], 71), 0),
        "grad_output": noise(streams_of[4], (TOKEN_COUNT, HEAD_COUNT * VALUE_HEAD_DIM), 4.0, 24.0, ((0, 32), (1, 32))),
    }


soft_scale = (1.0 + 0.1 * math.log(40.0)) ** 2 / math.sqrt(192.0)
epsilon = 1e-06

def head_backward(query_h, grad_h, key_nope, rotated_key_part, value):
    key_full = jnp.concatenate([key_nope, rotated_key_part], axis=1)
    seq_len = query_h.shape[0]
    scores = soft_scale * jnp.dot(query_h, key_full.T, preferred_element_type=jnp.float32)
    row_index = lax.broadcasted_iota(jnp.int32, (seq_len, seq_len), 0)
    col_index = lax.broadcasted_iota(jnp.int32, (seq_len, seq_len), 1)
    scores = jnp.where(col_index <= row_index, scores, -jnp.inf)
    row_max = lax.optimization_barrier(jnp.max(scores, axis=1, keepdims=True))
    weights = jnp.exp(scores - row_max)
    probs = weights / lax.optimization_barrier(jnp.sum(weights, axis=1, keepdims=True))
    prob_low = probs.astype(jnp.bfloat16)
    grad_value = jnp.dot(prob_low.T, grad_h, preferred_element_type=jnp.float32)
    grad_probs = jnp.dot(grad_h, value.T, preferred_element_type=jnp.float32)
    row_delta = lax.optimization_barrier(jnp.sum(probs * grad_probs, axis=1, keepdims=True))
    grad_scores = (soft_scale * probs * (grad_probs - row_delta)).astype(jnp.bfloat16)
    grad_query = jnp.dot(grad_scores, key_full, preferred_element_type=jnp.float32).astype(jnp.bfloat16)
    grad_key = jnp.dot(grad_scores.T, query_h, preferred_element_type=jnp.float32)
    grad_up_h = jnp.concatenate([grad_key[:, :PLAIN_HEAD_DIM], grad_value], axis=1).astype(jnp.bfloat16)
    return (grad_query, grad_up_h, grad_key[:, PLAIN_HEAD_DIM:])

def reference(latent_with_rope, latent_norm_weight, expand_weight, queries, grad_output):
    latent_state = latent_with_rope[:, :KEY_VALUE_RANK].astype(jnp.float32)
    rotated_key_part = latent_with_rope[:, KEY_VALUE_RANK:]
    inverse = lax.rsqrt(lax.optimization_barrier(jnp.mean(latent_state * latent_state, axis=1, keepdims=True)) + epsilon)
    unit = latent_state * inverse
    normed = (unit * latent_norm_weight).astype(jnp.bfloat16)
    projected = jnp.dot(normed, expand_weight, preferred_element_type=jnp.float32).astype(jnp.bfloat16)
    sequences = TOKEN_COUNT // SEQ
    up_blocks = projected.reshape(sequences, SEQ, HEAD_COUNT, PLAIN_HEAD_DIM + VALUE_HEAD_DIM)
    query_blocks = queries.reshape(sequences, SEQ, HEAD_COUNT, PLAIN_HEAD_DIM + ROPE)
    grad_blocks = grad_output.reshape(sequences, SEQ, HEAD_COUNT, VALUE_HEAD_DIM)
    rope_blocks = rotated_key_part.reshape(sequences, SEQ, ROPE)

    def one_sequence(operands):
        up_s, query_s, grad_s, rope_s = operands

        def one_head(head_operands):
            up_h, query_h, grad_h = head_operands
            return head_backward(query_h, grad_h, up_h[:, :PLAIN_HEAD_DIM], rope_s, up_h[:, PLAIN_HEAD_DIM:])
        grad_query, grad_up_h, grad_rope_h = lax.map(one_head, (up_s.transpose(1, 0, 2), query_s.transpose(1, 0, 2), grad_s.transpose(1, 0, 2)))
        return (grad_query, grad_up_h, lax.optimization_barrier(jnp.sum(grad_rope_h, axis=0)))
    grad_query, grad_up, grad_rope = lax.map(one_sequence, (up_blocks, query_blocks, grad_blocks, rope_blocks))
    grad_queries = grad_query.transpose(0, 2, 1, 3).reshape(TOKEN_COUNT, HEAD_COUNT * (PLAIN_HEAD_DIM + ROPE))
    grad_up = grad_up.transpose(0, 2, 1, 3).reshape(TOKEN_COUNT, HEAD_COUNT * (PLAIN_HEAD_DIM + VALUE_HEAD_DIM))
    grad_rope = grad_rope.reshape(TOKEN_COUNT, ROPE)
    grad_up_weight = jnp.dot(normed.T, grad_up, preferred_element_type=jnp.float32)
    grad_normed = jnp.dot(grad_up, expand_weight.T, preferred_element_type=jnp.float32)
    grad_gain = lax.optimization_barrier(jnp.sum(grad_normed * unit, axis=0))
    scaled = grad_normed * latent_norm_weight
    grad_latent = inverse * (scaled - unit * lax.optimization_barrier(jnp.mean(scaled * unit, axis=1, keepdims=True)))
    grad_joint_latent = jnp.concatenate([grad_latent, grad_rope], axis=1).astype(jnp.bfloat16)
    return (grad_queries, grad_joint_latent, grad_up_weight, grad_gain)
```

```python
import functools
import math

import jax
import jax.numpy as jnp
from jax import lax
from jax.experimental import pallas as pl
from jax.experimental.pallas import tpu as pltpu
from jax.sharding import PartitionSpec as P

ROPE = 64
NOPE = 128
VALUE = 128
LATENT = 512
JOINT = LATENT + ROPE
SEQ = 512
HALF = SEQ // 2
CHUNK = 16
NX, NY, NCORE = 4, 4, 2
NZ, NLO = 16, 2

soft_scale = (1.0 + 0.1 * math.log(40.0)) ** 2 / math.sqrt(192.0)
exp2_scale = soft_scale * math.log2(math.e)
epsilon = 1e-06

F32 = jnp.float32
BF16 = jnp.bfloat16
MESH = pl.DeviceIdType.MESH


def dot(a, b, contract):
    return lax.dot_general(a, b, (contract, ((), ())), preferred_element_type=F32)


def head_probs(scores, grads):
    keep = lax.broadcasted_iota(jnp.int32, (HALF, HALF), 0) <= lax.broadcasted_iota(
        jnp.int32, (HALF, HALF), 1
    )
    scores = scores[:-1] + [jnp.where(keep, scores[-1], -jnp.inf)]
    top = functools.reduce(
        jnp.maximum, [jnp.max(block, axis=0, keepdims=True) for block in scores]
    )
    shift = top * exp2_scale
    weights = [jnp.exp2(block * exp2_scale - shift) for block in scores]
    total = sum(jnp.sum(block, axis=0, keepdims=True) for block in weights)
    inverse = 1.0 / total
    probs = [block * inverse for block in weights]
    delta = sum(
        jnp.sum(prob * grad, axis=0, keepdims=True) for prob, grad in zip(probs, grads)
    )
    grad_scores = [
        (prob * (grad - delta) * soft_scale).astype(BF16) for prob, grad in zip(probs, grads)
    ]
    return [prob.astype(BF16) for prob in probs], grad_scores


def compute_body(lat, weight, expand, query, grad_out, grad_query, joint_part, gain_part,
                 up_part, unit, normed, normed_t, rope_pad, rope_sum, grad_up, key_pad, value,
                 probs, grad_scores):
    heads = expand.shape[1] // (NOPE + VALUE)
    state = lat[:, :LATENT].astype(F32)
    inverse = lax.rsqrt(jnp.mean(state * state, axis=1, keepdims=True) + epsilon)
    unit[...] = state * inverse
    scaled = unit[...] * weight[...]
    normed[...] = scaled.astype(BF16)
    normed_t[...] = scaled.T.astype(BF16)
    rope_pad[...] = jnp.zeros_like(rope_pad)
    rope_pad[:, :ROPE] = lat[:, LATENT:].astype(F32)
    rope_sum[...] = jnp.zeros_like(rope_sum)

    low, high, whole = slice(0, HALF), slice(HALF, SEQ), slice(0, SEQ)
    for head in range(heads):
        odd = head % 2
        columns = slice(head * 256, (head + 1) * 256)
        wide = slice((head // 2) * 384 + odd * 128, (head // 2) * 384 + odd * 128 + 256)
        own = slice(head * VALUE, (head + 1) * VALUE)
        projected = dot(normed[...], expand[:, columns], ((1,), (0,)))
        value[...] = projected[:, NOPE:].astype(BF16)
        keys = jnp.concatenate([projected[:, :NOPE], rope_pad[...]], axis=1)
        if odd:
            keys = pltpu.roll(keys, 64, 1)
        key_pad[...] = keys.astype(BF16)
        for rows, blocks in ((low, (low,)), (high, (low, high))):
            scores = [dot(key_pad[b, :], query[rows, wide], ((1,), (1,))) for b in blocks]
            grads = [dot(value[b, :], grad_out[rows, own], ((1,), (1,))) for b in blocks]
            prob, grad_score = head_probs(scores, grads)
            for b, p, g in zip(blocks, prob, grad_score):
                probs[b, rows] = p
                grad_scores[b, rows] = g
        out_low = dot(grad_scores[low, low], key_pad[low, :], ((0,), (0,)))
        out_high = dot(grad_scores[:, high], key_pad[...], ((0,), (0,)))
        base = (head // 2) * 384
        for rows, out in ((low, out_low), (high, out_high)):
            if odd:
                grad_query[rows, base + 128:base + 256] = (
                    grad_query[rows, base + 128:base + 256] + out[:, :128].astype(BF16)
                )
                grad_query[rows, base + 256:base + 384] = out[:, 128:].astype(BF16)
            else:
                grad_query[rows, base:base + 256] = out.astype(BF16)
        for rows, used in ((low, whole), (high, high)):
            grad_key = dot(grad_scores[rows, used], query[used, wide], ((1,), (0,)))
            grad_value = dot(probs[rows, used], grad_out[used, own], ((1,), (0,)))
            if odd:
                grad_key = pltpu.roll(grad_key, 192, 1)
            grad_up[rows, head * 256:head * 256 + NOPE] = grad_key[:, :NOPE].astype(BF16)
            grad_up[rows, head * 256 + NOPE:(head + 1) * 256] = grad_value.astype(BF16)
            rope_sum[rows, :] += grad_key[:, NOPE:]

    gain = jnp.zeros((1, LATENT), F32)
    for quarter in range(4):
        rows = slice(quarter * 128, (quarter + 1) * 128)
        grad_normed = dot(grad_up[rows, :], expand[...], ((1,), (1,)))
        gain = gain + jnp.sum(grad_normed * unit[rows, :], axis=0, keepdims=True)
        joint_part[quarter, :, :, :, :LATENT] = grad_normed.astype(BF16).reshape(
            2, 4, CHUNK, LATENT
        )
        joint_part[quarter, :, :, :, LATENT:] = rope_sum[rows, :ROPE].astype(BF16).reshape(
            2, 4, CHUNK, ROPE
        )
    gain_part[...] = jnp.zeros_like(gain_part)
    for piece in range(4):
        gain_part[piece:piece + 1, :] = gain[:, piece * 128:(piece + 1) * 128]
    for head in range(heads):
        columns = slice(head * 256, (head + 1) * 256)
        up_part[:, :, :, columns] = (
            dot(normed_t[...], grad_up[:, columns], ((1,), (0,)))
            .astype(BF16)
            .reshape(16, 2, CHUNK, 256)
        )


def comm_body(lat, weight, joint_part, gain_part, up_part, joint, up, gain_out,
              lo_in, lo_sum, near_in, near_sum, far_in, core_in, core_sum, x_in, y_sum, y_in,
              gain_lo, gain_core, gain_far, gain_near, gain_x, gain_y,
              lo_sem, near_sem, far_sem, core_sem, x_sem, y_sem, out_far_sem, out_near_sem,
              out_lo_sem, gain_pair_sem, gain_quad_sem):
    d, t = lax.axis_index("dp"), lax.axis_index("tensor")
    core, y, x = d % 2, (d // 2) % 4, d // 8
    lo, z = t % 2, t // 2
    quarter, phase = z // 4, z % 4

    def at_z(other):
        return (d, other * 2 + lo)

    def z_plus(step):
        return at_z((z + (step + NZ)) % NZ)

    lo_peer = (d, t + 1 - 2 * lo)
    core_peer = (d + 1 - 2 * core, t)
    x_peers = [((((x + j) % 4) * 4 + y) * 2 + core, t) for j in (1, 2, 3)]
    y_peers = [((x * 4 + (y + j) % 4) * 2 + core, t) for j in (1, 2, 3)]
    far_peers = [z_plus(4 * j) for j in (1, 2, 3)]
    near_peers = {s: z_plus(s) for s in (1, -1, 2, -2)}

    barrier = pltpu.get_barrier_semaphore()
    peers = [lo_peer, core_peer] + x_peers + y_peers + far_peers + list(near_peers.values())
    for peer in peers:
        pl.semaphore_signal(barrier, inc=1, device_id=peer, device_id_type=MESH)
    pl.semaphore_wait(barrier, len(peers))

    started = []

    def send(src, dst, sems, slot, recv_slot, peer):
        copy = pltpu.make_async_remote_copy(
            src_ref=src, dst_ref=dst, send_sem=sems.at[(0,) + slot],
            recv_sem=sems.at[(1,) + recv_slot], device_id=peer, device_id_type=MESH,
        )
        copy.start()
        started.append(copy)

    def arrive(dst, sems, recv_slot, peer):
        pltpu.make_async_remote_copy(
            src_ref=dst, dst_ref=dst, send_sem=sems.at[(0,) + recv_slot],
            recv_sem=sems.at[(1,) + recv_slot], device_id=peer, device_id_type=MESH,
        ).wait_recv()

    def gain_pair_send(value, slots, index, me, peer):
        slots[me] = value
        send(slots.at[me], slots.at[me], gain_pair_sem, (index,), (index,), peer)

    def gain_pair_sum(slots, index, me, peer):
        arrive(slots.at[1 - me], gain_pair_sem, (index,), peer)
        return slots[0] + slots[1]

    def gain_quad_send(value, slots, index, me, peers_of):
        slots[me] = value
        for j, peer in enumerate(peers_of):
            send(slots.at[me], slots.at[me], gain_quad_sem, (index, j), (index, j), peer)

    def gain_quad_sum(slots, index, me, steps, peers_of):
        for j, (step, peer) in enumerate(zip(steps, peers_of)):
            arrive(slots.at[(me + (4 - step)) % 4], gain_quad_sem, (index, j), peer)
        return (slots[0] + slots[1]) + (slots[2] + slots[3])

    for a in range(4):
        send(joint_part.at[a, 1 - lo], lo_in.at[a], lo_sem, (a,), (a,), lo_peer)
    gain_pair_send(gain_part[...], gain_lo, 0, lo, lo_peer)
    for i in range(4):
        send(up_part.at[pl.ds(4 * i, 4), 1 - core], core_in.at[pl.ds(4 * i, 4)], core_sem,
             (i,), (i,), core_peer)

    for a in range(4):
        arrive(lo_in.at[a], lo_sem, (a,), lo_peer)
        lo_sum[a] = (joint_part[a, lo].astype(F32) + lo_in[a].astype(F32)).astype(BF16)
        for i, step in enumerate((1, -1, 2 if a < 2 else -2)):
            other = (phase + (step + 4)) % 4
            send(lo_sum.at[a, other], near_in.at[i, a], near_sem, (i, a), (i, a),
                 near_peers[step])
    gain_value = gain_pair_sum(gain_lo, 0, lo, lo_peer)
    gain_pair_send(gain_value, gain_core, 1, core, core_peer)

    for i in range(4):
        arrive(core_in.at[pl.ds(4 * i, 4)], core_sem, (i,), core_peer)
    for j in (1, 2, 3, 0):
        rows = pl.ds(((x + j) % 4) * 4, 4)
        core_sum[rows] = (
            up_part[rows, core].astype(F32) + core_in[rows].astype(F32)
        ).astype(BF16)
        if j:
            send(core_sum.at[rows], x_in.at[j - 1], x_sem, (j - 1,), (j - 1,), x_peers[j - 1])

    for a in range(4):
        for i, step in enumerate((1, -1, 2 if a < 2 else -2)):
            arrive(near_in.at[i, a], near_sem, (i, a), near_peers[-step])
        near_sum[a] = (
            (lo_sum[a, phase].astype(F32) + near_in[0, a].astype(F32))
            + (near_in[1, a].astype(F32) + near_in[2, a].astype(F32))
        ).astype(BF16)
    for j in (1, 2, 3):
        send(near_sum.at[(quarter + j) % 4], far_in.at[j - 1], far_sem, (j - 1,), (j - 1,),
             far_peers[j - 1])
    gain_value = gain_pair_sum(gain_core, 1, core, core_peer)
    gain_quad_send(gain_value, gain_far, 0, quarter, far_peers)

    for j in (1, 2, 3):
        arrive(x_in.at[j - 1], x_sem, (j - 1,), x_peers[3 - j])
    y_sum[...] = (
        (core_sum[pl.ds(x * 4, 4)].astype(F32) + x_in[0].astype(F32))
        + (x_in[1].astype(F32) + x_in[2].astype(F32))
    ).astype(BF16)
    for j in (1, 2, 3):
        send(y_sum.at[(y + j) % 4], y_in.at[j - 1], y_sem, (j - 1,), (j - 1,), y_peers[j - 1])

    first = pl.multiple_of(quarter * 128 + lo * 64 + phase * CHUNK, CHUNK)
    state = lat[pl.ds(first, CHUNK), :LATENT].astype(F32)
    inverse = lax.rsqrt(jnp.mean(state * state, axis=1, keepdims=True) + epsilon)
    unit = state * inverse
    for j in (1, 2, 3):
        arrive(far_in.at[j - 1], far_sem, (j - 1,), far_peers[3 - j])
    total = (near_sum[quarter].astype(F32) + far_in[0].astype(F32)) + (
        far_in[1].astype(F32) + far_in[2].astype(F32)
    )
    scaled = total[:, :LATENT] * weight[...]
    grad_latent = inverse * (scaled - unit * jnp.mean(scaled * unit, axis=1, keepdims=True))
    joint[quarter, lo, phase, :, :LATENT] = grad_latent.astype(BF16)
    joint[quarter, lo, phase, :, LATENT:] = total[:, LATENT:].astype(BF16)
    for j in (1, 2, 3):
        mine = joint.at[quarter, lo, phase]
        send(mine, mine, out_far_sem, (j - 1,), (j - 1,), far_peers[j - 1])
    gain_value = gain_quad_sum(gain_far, 0, quarter, (1, 2, 3), far_peers[::-1])
    gain_near_peers = [near_peers[1], near_peers[-1], near_peers[2]]
    gain_quad_send(gain_value, gain_near, 1, phase, gain_near_peers)

    for j in (1, 2, 3):
        arrive(y_in.at[j - 1], y_sem, (j - 1,), y_peers[3 - j])
    up[...] = (y_sum[y].astype(F32) + y_in[0].astype(F32)) + (
        y_in[1].astype(F32) + y_in[2].astype(F32)
    )

    for j in (1, 2, 3):
        theirs = joint.at[(quarter + (4 - j)) % 4, lo, phase]
        arrive(theirs, out_far_sem, (j - 1,), far_peers[3 - j])
    for i, step in enumerate((1, -1)):
        mine = joint.at[:, lo, phase]
        send(mine, mine, out_near_sem, (i,), (i,), near_peers[step])
    for i, step in enumerate((2, -2)):
        mine = joint.at[pl.ds(2 * i, 2), lo, phase]
        send(mine, mine, out_near_sem, (2 + i,), (2 + i,), near_peers[step])
    mine = joint.at[:, lo, phase]
    send(mine, mine, out_lo_sem, (0,), (0,), lo_peer)
    gain_value = gain_quad_sum(
        gain_near, 1, phase, (1, 3, 2), [near_peers[-1], near_peers[1], near_peers[-2]]
    )
    gain_quad_send(gain_value, gain_x, 2, x, x_peers)

    for i, step in enumerate((1, -1, 2)):
        other = (phase + (4 - step)) % 4
        theirs = joint.at[:, lo, other]
        if i < 2:
            arrive(theirs, out_near_sem, (i,), near_peers[-step])
        else:
            arrive(joint.at[pl.ds(0, 2), lo, other], out_near_sem, (2,), near_peers[-2])
            arrive(joint.at[pl.ds(2, 2), lo, other], out_near_sem, (3,), near_peers[2])
        send(theirs, theirs, out_lo_sem, (1 + i,), (1 + i,), lo_peer)
    gain_value = gain_quad_sum(gain_x, 2, x, (1, 2, 3), x_peers[::-1])
    gain_quad_send(gain_value, gain_y, 3, y, y_peers)
    gain_value = gain_quad_sum(gain_y, 3, y, (1, 2, 3), y_peers[::-1])
    for piece in range(4):
        gain_out[:, piece * 128:(piece + 1) * 128] = gain_value[piece:piece + 1, :]

    arrive(joint.at[:, 1 - lo, phase], out_lo_sem, (0,), lo_peer)
    for i, step in enumerate((1, -1, 2)):
        other = (phase + (4 - step)) % 4
        arrive(joint.at[:, 1 - lo, other], out_lo_sem, (1 + i,), lo_peer)
    for copy in started:
        copy.wait_send()


def vmem_spec():
    return pl.BlockSpec(memory_space=pltpu.VMEM)


def per_device(latent_with_rope, latent_norm_weight, expand_weight, queries, grad_output):
    width = expand_weight.shape[1]
    weight = latent_norm_weight.reshape(1, LATENT)
    joint_shape = (4, 2, 4, CHUNK, JOINT)
    grad_queries, joint_part, gain_part, up_part = pl.pallas_call(
        compute_body,
        name="attention_backward",
        out_shape=(
            jax.ShapeDtypeStruct(queries.shape, BF16),
            jax.ShapeDtypeStruct(joint_shape, BF16),
            jax.ShapeDtypeStruct((8, 128), F32),
            jax.ShapeDtypeStruct((16, 2, CHUNK, width), BF16),
        ),
        in_specs=[vmem_spec()] * 5,
        out_specs=(vmem_spec(),) * 4,
        scratch_shapes=[
            pltpu.VMEM((SEQ, LATENT), F32),
            pltpu.VMEM((SEQ, LATENT), BF16),
            pltpu.VMEM((LATENT, SEQ), BF16),
            pltpu.VMEM((SEQ, 128), F32),
            pltpu.VMEM((SEQ, 128), F32),
            pltpu.VMEM((SEQ, width), BF16),
            pltpu.VMEM((SEQ, 256), BF16),
            pltpu.VMEM((SEQ, VALUE), BF16),
            pltpu.VMEM((SEQ, SEQ), BF16),
            pltpu.VMEM((SEQ, SEQ), BF16),
        ],
        compiler_params=pltpu.CompilerParams(vmem_limit_bytes=32 * 2**20),
    )(latent_with_rope, weight, expand_weight, queries, grad_output)

    sem = pltpu.SemaphoreType.DMA
    joint, up, gain = pl.pallas_call(
        comm_body,
        name="sums",
        out_shape=(
            jax.ShapeDtypeStruct(joint_shape, BF16),
            jax.ShapeDtypeStruct((CHUNK, width), F32),
            jax.ShapeDtypeStruct((1, LATENT), F32),
        ),
        in_specs=[vmem_spec()] * 5,
        out_specs=(vmem_spec(),) * 3,
        scratch_shapes=[
            pltpu.VMEM((4, 4, CHUNK, JOINT), BF16),
            pltpu.VMEM((4, 4, CHUNK, JOINT), BF16),
            pltpu.VMEM((3, 4, CHUNK, JOINT), BF16),
            pltpu.VMEM((4, CHUNK, JOINT), BF16),
            pltpu.VMEM((3, CHUNK, JOINT), BF16),
            pltpu.VMEM((16, CHUNK, width), BF16),
            pltpu.VMEM((16, CHUNK, width), BF16),
            pltpu.VMEM((3, 4, CHUNK, width), BF16),
            pltpu.VMEM((4, CHUNK, width), BF16),
            pltpu.VMEM((3, CHUNK, width), BF16),
            pltpu.VMEM((2, 8, 128), F32),
            pltpu.VMEM((2, 8, 128), F32),
            pltpu.VMEM((4, 8, 128), F32),
            pltpu.VMEM((4, 8, 128), F32),
            pltpu.VMEM((4, 8, 128), F32),
            pltpu.VMEM((4, 8, 128), F32),
            sem((2, 4)),
            sem((2, 3, 4)),
            sem((2, 3)),
            sem((2, 4)),
            sem((2, 3)),
            sem((2, 3)),
            sem((2, 3)),
            sem((2, 4)),
            sem((2, 4)),
            sem((2, 2)),
            sem((2, 4, 3)),
        ],
        compiler_params=pltpu.CompilerParams(
            collective_id=0, has_side_effects=True, vmem_limit_bytes=24 * 2**20
        ),
    )(latent_with_rope, weight, joint_part, gain_part, up_part)
    return (
        grad_queries,
        joint.reshape(SEQ, JOINT),
        up,
        gain.reshape(LATENT),
    )


def solution(mesh):
    assert mesh.shape["dp"] == NX * NY * NCORE and mesh.shape["tensor"] == NZ * NLO
    placed = (P("dp", None), P(), P(None, "tensor"), P("dp", "tensor"), P("dp", "tensor"))
    return jax.shard_map(
        per_device,
        mesh=mesh,
        in_specs=placed,
        out_specs=(P("dp", "tensor"), P("dp", None), P("dp", "tensor"), P()),
        check_vma=False,
    )
```

```python
import functools
import math

import jax
import jax.numpy as jnp
from jax import lax
from jax.experimental import pallas as pl
from jax.experimental.pallas import tpu as pltpu
from jax.sharding import PartitionSpec as P

ROPE = 64
NOPE = 128
VALUE = 128
LATENT = 512
JOINT = LATENT + ROPE
PADDED = LATENT + 128
SEQ = 512
HALF = SEQ // 2
CHUNK = 16
NX, NY, NCORE = 4, 4, 2
NZ, NLO = 16, 2

soft_scale = (1.0 + 0.1 * math.log(40.0)) ** 2 / math.sqrt(192.0)
exp2_scale = soft_scale * math.log2(math.e)
epsilon = 1e-06

F32 = jnp.float32
BF16 = jnp.bfloat16
MESH = pl.DeviceIdType.MESH


def dot(a, b, contract):
    return lax.dot_general(a, b, (contract, ((), ())), preferred_element_type=F32)


def head_probs(scores, grads):
    keep = lax.broadcasted_iota(jnp.int32, (HALF, HALF), 0) <= lax.broadcasted_iota(
        jnp.int32, (HALF, HALF), 1
    )
    scores = scores[:-1] + [jnp.where(keep, scores[-1], -jnp.inf)]
    top = functools.reduce(
        jnp.maximum, [jnp.max(block, axis=0, keepdims=True) for block in scores]
    )
    shift = top * exp2_scale
    weights = [jnp.exp2(block * exp2_scale - shift) for block in scores]
    total = sum(jnp.sum(block, axis=0, keepdims=True) for block in weights)
    inverse = 1.0 / total
    probs = [block * inverse for block in weights]
    delta = sum(
        jnp.sum(prob * grad, axis=0, keepdims=True) for prob, grad in zip(probs, grads)
    )
    grad_scores = [
        (prob * (grad - delta) * soft_scale).astype(BF16) for prob, grad in zip(probs, grads)
    ]
    return [prob.astype(BF16) for prob in probs], grad_scores


def transposed_rows(row):
    return jnp.broadcast_to(row, (128, row.shape[1])).T


def wide_columns(block):
    return jnp.concatenate([block] * (LATENT // 128), axis=1)


def attention_part(lat, weight, expand, query, grad_out, grad_query, joint_part, gain_part,
                   unit, inverse, normed, normed_t, rope_pad, rope_sum, grad_up, key_pad, value,
                   probs, grad_scores, loads):
    heads = expand.shape[1] // (NOPE + VALUE)
    loads[0].wait()
    loads[1].wait()
    state = lat[:LATENT, :].astype(F32)
    inverse_row = lax.rsqrt(jnp.mean(state * state, axis=0, keepdims=True) + epsilon)
    unit_t = state * inverse_row
    inverse[...] = transposed_rows(inverse_row)
    unit[...] = unit_t.T
    normed[...] = (unit[...] * weight[...]).astype(BF16)
    normed_t[...] = (unit_t * wide_columns(transposed_rows(weight[...]))).astype(BF16)
    rope_pad[...] = jnp.concatenate(
        [lat[LATENT:, :].astype(F32), jnp.zeros((128 - ROPE, SEQ), F32)], axis=0
    ).T
    rope_sum[...] = jnp.zeros_like(rope_sum)

    low, high, whole = slice(0, HALF), slice(HALF, SEQ), slice(0, SEQ)
    loads[2].wait()
    for head in range(heads):
        odd = head % 2
        columns = slice(head * 256, (head + 1) * 256)
        wide = slice((head // 2) * 384 + odd * 128, (head // 2) * 384 + odd * 128 + 256)
        own = slice(head * VALUE, (head + 1) * VALUE)
        projected = dot(normed[...], expand[:, columns], ((1,), (0,)))
        value[...] = projected[:, NOPE:].astype(BF16)
        keys = jnp.concatenate([projected[:, :NOPE], rope_pad[...]], axis=1)
        if odd:
            keys = pltpu.roll(keys, 64, 1)
        key_pad[...] = keys.astype(BF16)
        if head == 0:
            loads[3].wait()
            loads[4].wait()
        for rows, blocks in ((low, (low,)), (high, (low, high))):
            scores = [dot(key_pad[b, :], query[rows, wide], ((1,), (1,))) for b in blocks]
            grads = [dot(value[b, :], grad_out[rows, own], ((1,), (1,))) for b in blocks]
            prob, grad_score = head_probs(scores, grads)
            for b, p, g in zip(blocks, prob, grad_score):
                probs[b, rows] = p
                grad_scores[b, rows] = g
        out_low = dot(grad_scores[low, low], key_pad[low, :], ((0,), (0,)))
        out_high = dot(grad_scores[:, high], key_pad[...], ((0,), (0,)))
        base = (head // 2) * 384
        for rows, out in ((low, out_low), (high, out_high)):
            if odd:
                grad_query[rows, base + 128:base + 256] = (
                    grad_query[rows, base + 128:base + 256] + out[:, :128].astype(BF16)
                )
                grad_query[rows, base + 256:base + 384] = out[:, 128:].astype(BF16)
            else:
                grad_query[rows, base:base + 256] = out.astype(BF16)
        for rows, used in ((low, whole), (high, high)):
            grad_key = dot(grad_scores[rows, used], query[used, wide], ((1,), (0,)))
            grad_value = dot(probs[rows, used], grad_out[used, own], ((1,), (0,)))
            if odd:
                grad_key = pltpu.roll(grad_key, 192, 1)
            grad_up[rows, head * 256:head * 256 + NOPE] = grad_key[:, :NOPE].astype(BF16)
            grad_up[rows, head * 256 + NOPE:(head + 1) * 256] = grad_value.astype(BF16)
            rope_sum[rows, :] += grad_key[:, NOPE:]

    gain = jnp.zeros((1, LATENT), F32)
    for part in range(4):
        rows = slice(part * 128, (part + 1) * 128)
        grad_normed = dot(grad_up[rows, :], expand[...], ((1,), (1,)))
        gain = gain + jnp.sum(grad_normed * unit[rows, :], axis=0, keepdims=True)
        joint_part[part, :, :, :, :LATENT] = grad_normed.astype(BF16).reshape(
            2, 4, CHUNK, LATENT
        )
        joint_part[part, :, :, :, LATENT:] = rope_sum[rows, :].astype(BF16).reshape(
            2, 4, CHUNK, 128
        )
    gain_part[...] = jnp.zeros_like(gain_part)
    for piece in range(4):
        gain_part[piece:piece + 1, :] = gain[:, piece * 128:(piece + 1) * 128]


def up_gradient(normed_t, grad_up, up_part):
    for head in range(grad_up.shape[1] // 256):
        columns = slice(head * 256, (head + 1) * 256)
        up_part[:, :, :, columns] = (
            dot(normed_t[...], grad_up[:, columns], ((1,), (0,)))
            .astype(BF16)
            .reshape(16, 2, CHUNK, 256)
        )


def body(lat_hbm, weight_hbm, expand_hbm, query_hbm, grad_out_hbm,
         grad_query_hbm, joint_hbm, up_hbm, gain_hbm,
         lat, weight, expand, query, grad_out, load_sem, grad_query, joint, up, gain_out, save_sem,
         unit, inverse, normed, normed_t, rope_pad, rope_sum, grad_up, key_pad, value, probs,
         grad_scores, joint_part, gain_part, up_part,
         lo_in, lo_sum, near_in, near_sum, far_in, core_in, core_sum, x_in, y_sum, y_in,
         gain_lo, gain_core, gain_far, gain_near, gain_x, gain_y,
         lo_sem, near_sem, far_sem, core_sem, x_sem, y_sem, out_far_sem, out_near_sem,
         out_lo_sem, gain_pair_sem, gain_quad_sem):
    d, t = lax.axis_index("dp"), lax.axis_index("tensor")
    core, y, x = d % 2, (d // 2) % 4, d // 8
    lo, z = t % 2, t // 2
    quarter, phase = z // 4, z % 4

    def z_plus(step):
        return (d, ((z + step + NZ) % NZ) * 2 + lo)

    lo_peer = (d, t + 1 - 2 * lo)
    core_peer = (d + 1 - 2 * core, t)
    x_peers = [((((x + j) % 4) * 4 + y) * 2 + core, t) for j in (1, 2, 3)]
    y_peers = [((x * 4 + (y + j) % 4) * 2 + core, t) for j in (1, 2, 3)]
    far_peers = [z_plus(4 * j) for j in (1, 2, 3)]
    near_peers = {s: z_plus(s) for s in (1, -1, 2, -2)}

    barrier = pltpu.get_barrier_semaphore()
    peers = far_peers + [lo_peer, core_peer] + x_peers + y_peers + list(near_peers.values())
    for peer in peers:
        pl.semaphore_signal(barrier, inc=1, device_id=peer, device_id_type=MESH)

    loads = []
    for i, (src, dst) in enumerate(
        ((lat_hbm, lat), (weight_hbm, weight), (expand_hbm, expand), (query_hbm, query),
         (grad_out_hbm, grad_out))
    ):
        loads.append(pltpu.make_async_copy(src, dst, load_sem.at[i]))
        loads[-1].start()

    attention_part(lat, weight, expand, query, grad_out, grad_query, joint_part, gain_part,
                   unit, inverse, normed, normed_t, rope_pad, rope_sum, grad_up, key_pad, value,
                   probs, grad_scores, loads)
    saves = [pltpu.make_async_copy(grad_query, grad_query_hbm, save_sem.at[0])]
    saves[0].start()

    pl.semaphore_wait(barrier, len(peers))

    started = []

    def send(src, dst, sems, slot, recv_slot, peer):
        copy = pltpu.make_async_remote_copy(
            src_ref=src, dst_ref=dst, send_sem=sems.at[(0,) + slot],
            recv_sem=sems.at[(1,) + recv_slot], device_id=peer, device_id_type=MESH,
        )
        copy.start()
        started.append(copy)

    def arrive(dst, sems, recv_slot, peer):
        pltpu.make_async_remote_copy(
            src_ref=dst, dst_ref=dst, send_sem=sems.at[(0,) + recv_slot],
            recv_sem=sems.at[(1,) + recv_slot], device_id=peer, device_id_type=MESH,
        ).wait_recv()

    def gain_pair_send(value, slots, index, me, peer):
        slots[me] = value
        send(slots.at[me], slots.at[me], gain_pair_sem, (index,), (index,), peer)

    def gain_pair_sum(slots, index, me, peer):
        arrive(slots.at[1 - me], gain_pair_sem, (index,), peer)
        return slots[0] + slots[1]

    def gain_quad_send(value, slots, index, me, peers_of):
        slots[me] = value
        for j, peer in enumerate(peers_of):
            send(slots.at[me], slots.at[me], gain_quad_sem, (index, j), (index, j), peer)

    def gain_quad_sum(slots, index, me, steps, peers_of):
        for j, (step, peer) in enumerate(zip(steps, peers_of)):
            arrive(slots.at[(me + (4 - step)) % 4], gain_quad_sem, (index, j), peer)
        return (slots[0] + slots[1]) + (slots[2] + slots[3])

    order = (2, 1, 3, 0)
    deltas = (0, 1, -1, 2)
    slot_of = {1: 0, -1: 1, 2: 2}

    def collected(step, delta):
        holder = quarter if delta in (0, 2) else ((z + delta + NZ) % NZ) // 4
        return (holder + step) % 4, (phase + delta + 4) % 4

    def two_away(a):
        return 2 - 4 * (a // 2)

    gain_pair_send(gain_part[...], gain_lo, 0, lo, lo_peer)
    for step in order:
        for delta in deltas:
            a, k = collected(step, delta)
            send(joint_part.at[a, 1 - lo, k], lo_in.at[a, k], lo_sem, (a, k), (a, k), lo_peer)

    up_gradient(normed_t, grad_up, up_part)
    for i in range(4):
        send(up_part.at[pl.ds(4 * i, 4), 1 - core], core_in.at[pl.ds(4 * i, 4)], core_sem,
             (i,), (i,), core_peer)

    def lo_step(step):
        for delta in deltas:
            a, k = collected(step, delta)
            arrive(lo_in.at[a, k], lo_sem, (a, k), lo_peer)
            lo_sum[a, k] = (
                joint_part[a, lo, k].astype(F32) + lo_in[a, k].astype(F32)
            ).astype(BF16)
            if delta:
                slot = slot_of[delta]
                peer = z_plus(two_away(a)) if delta == 2 else near_peers[delta]
                send(lo_sum.at[a, k], near_in.at[slot, a], near_sem, (slot, a), (slot, a), peer)

    def near_step(step):
        a = (quarter + step) % 4
        for delta in deltas[1:]:
            slot = slot_of[delta]
            arrive(near_in.at[slot, a], near_sem, (slot, a), near_peers[-delta])
        near_sum[a] = (
            (lo_sum[a, phase].astype(F32) + near_in[0, a].astype(F32))
            + (near_in[1, a].astype(F32) + near_in[2, a].astype(F32))
        ).astype(BF16)
        if step:
            send(near_sum.at[a], far_in.at[step - 1], far_sem, (step - 1,), (step - 1,),
                 far_peers[step - 1])

    lo_step(order[0])
    gain_value = gain_pair_sum(gain_lo, 0, lo, lo_peer)
    gain_pair_send(gain_value, gain_core, 1, core, core_peer)
    lo_step(order[1])
    gain_value = gain_pair_sum(gain_core, 1, core, core_peer)
    gain_quad_send(gain_value, gain_far, 0, quarter, far_peers)

    for i in range(4):
        arrive(core_in.at[pl.ds(4 * i, 4)], core_sem, (i,), core_peer)
    for j in (2, 1, 3, 0):
        rows = pl.ds(((x + j) % 4) * 4, 4)
        core_sum[rows] = (
            up_part[rows, core].astype(F32) + core_in[rows].astype(F32)
        ).astype(BF16)
        if j:
            send(core_sum.at[rows], x_in.at[j - 1], x_sem, (j - 1,), (j - 1,), x_peers[j - 1])

    near_step(order[0])
    lo_step(order[2])
    near_step(order[1])
    lo_step(order[3])
    near_step(order[2])
    near_step(order[3])
    gain_value = gain_quad_sum(gain_far, 0, quarter, (1, 2, 3), far_peers[::-1])
    gain_near_peers = [near_peers[1], near_peers[-1], near_peers[2]]
    gain_quad_send(gain_value, gain_near, 1, phase, gain_near_peers)

    first = pl.multiple_of(quarter * 128 + lo * 64 + phase * CHUNK, CHUNK)
    own_unit = unit[pl.ds(first, CHUNK), :]
    own_inverse = wide_columns(inverse[pl.ds(first, CHUNK), :])
    for j in (1, 3, 2):
        arrive(far_in.at[j - 1], far_sem, (j - 1,), far_peers[3 - j])
    total = (near_sum[quarter].astype(F32) + far_in[0].astype(F32)) + (
        far_in[1].astype(F32) + far_in[2].astype(F32)
    )
    scaled = total[:, :LATENT] * weight[...]
    grad_latent = own_inverse * (
        scaled - own_unit * jnp.mean(scaled * own_unit, axis=1, keepdims=True)
    )
    joint[quarter, lo, phase, :, :LATENT] = grad_latent.astype(BF16)
    joint[quarter, lo, phase, :, LATENT:] = total[:, LATENT:].astype(BF16)

    def to_lo(a, k):
        chunk = joint.at[a, lo, k]
        return pltpu.make_async_remote_copy(
            src_ref=chunk, dst_ref=chunk, send_sem=out_lo_sem.at[0, a, k],
            recv_sem=out_lo_sem.at[1, a, k], device_id=lo_peer, device_id_type=MESH,
        )

    def pass_on(a, k):
        to_lo(a, k).start()

    def spread(step):
        a = (quarter + 4 - step) % 4
        chunk = joint.at[a, lo, phase]
        if step:
            arrive(chunk, out_far_sem, (step - 1,), far_peers[3 - step])
        else:
            for j in (2, 1, 3):
                send(chunk, chunk, out_far_sem, (j - 1,), (j - 1,), far_peers[j - 1])
        for slot, peer in ((2, z_plus(two_away(a))), (0, near_peers[1]), (1, near_peers[-1])):
            send(chunk, chunk, out_near_sem, (slot, a), (slot, a), peer)
        pass_on(a, phase)

    def from_near(step):
        for delta in (1, -1, 2, -2):
            a = (((z - delta + NZ) % NZ) // 4 + 4 - step) % 4
            k = (phase - delta + 4) % 4
            slot = 2 if abs(delta) == 2 else slot_of[delta]

            def relay(a=a, k=k, slot=slot, delta=delta):
                arrive(joint.at[a, lo, k], out_near_sem, (slot, a), near_peers[-delta])
                pass_on(a, k)

            if slot < 2:
                relay()
            else:
                pl.when(a < 2 if delta == 2 else a >= 2)(relay)

    spread(0)
    gain_value = gain_quad_sum(
        gain_near, 1, phase, (1, 3, 2), [near_peers[-1], near_peers[1], near_peers[-2]]
    )
    gain_quad_send(gain_value, gain_x, 2, x, x_peers)
    for j in (1, 3, 2):
        arrive(x_in.at[j - 1], x_sem, (j - 1,), x_peers[3 - j])
    y_sum[...] = (
        (core_sum[pl.ds(x * 4, 4)].astype(F32) + x_in[0].astype(F32))
        + (x_in[1].astype(F32) + x_in[2].astype(F32))
    ).astype(BF16)
    for j in (2, 1, 3):
        send(y_sum.at[(y + j) % 4], y_in.at[j - 1], y_sem, (j - 1,), (j - 1,), y_peers[j - 1])
    from_near(0)
    gain_value = gain_quad_sum(gain_x, 2, x, (1, 2, 3), x_peers[::-1])
    gain_quad_send(gain_value, gain_y, 3, y, y_peers)
    spread(1)
    spread(3)
    from_near(1)
    from_near(3)
    spread(2)
    for j in (1, 3, 2):
        arrive(y_in.at[j - 1], y_sem, (j - 1,), y_peers[3 - j])
    up[...] = (y_sum[y].astype(F32) + y_in[0].astype(F32)) + (
        y_in[1].astype(F32) + y_in[2].astype(F32)
    )
    saves.append(pltpu.make_async_copy(up, up_hbm, save_sem.at[1]))
    saves[-1].start()
    from_near(2)
    gain_value = gain_quad_sum(gain_y, 3, y, (1, 2, 3), y_peers[::-1])
    for piece in range(4):
        gain_out[:, piece * 128:(piece + 1) * 128] = gain_value[piece:piece + 1, :]
    saves.append(pltpu.make_async_copy(gain_out, gain_hbm, save_sem.at[2]))
    saves[-1].start()
    for a in range(4):
        for k in range(4):
            arrive(joint.at[a, 1 - lo, k], out_lo_sem, (a, k), lo_peer)
    saves.append(pltpu.make_async_copy(joint, joint_hbm, save_sem.at[3]))
    saves[-1].start()
    for a in range(4):
        for k in range(4):
            to_lo(a, k).wait_send()
    for copy in started:
        copy.wait_send()
    for save in saves:
        save.wait()


def write_body(grad_query_in, joint_in, up_in, gain_in, grad_query_out, joint_out, up_out, gain_out,
               grad_query, joint, up, gain, joint_t, sems):
    def copies(pairs, first):
        return [
            pltpu.make_async_copy(src, dst, sems.at[first + i]) for i, (src, dst) in enumerate(pairs)
        ]

    reads = copies(
        ((joint_in, joint), (grad_query_in, grad_query), (up_in, up), (gain_in, gain)), 0
    )
    writes = copies(
        ((joint_t, joint_out), (grad_query, grad_query_out), (up, up_out), (gain, gain_out)), 4
    )
    for copy in reads:
        copy.start()
    reads[0].wait()
    for part in range(4):
        rows = joint[part].reshape(128, PADDED)
        joint_t[:, part * 128:(part + 1) * 128] = rows.astype(F32).T[:JOINT, :].astype(BF16)
    writes[0].start()
    for read, write in zip(reads[1:], writes[1:]):
        read.wait()
        write.start()
    for copy in writes:
        copy.wait()


def hbm_spec():
    return pl.BlockSpec(memory_space=pltpu.HBM)


def per_device(latent_with_rope, latent_norm_weight, expand_weight, queries, grad_output):
    width = expand_weight.shape[1]
    sem = pltpu.SemaphoreType.DMA
    joint_shape = (4, 2, 4, CHUNK, PADDED)
    grad_query, joint, up, gain = pl.pallas_call(
        body,
        name="attention_and_sums",
        out_shape=(
            jax.ShapeDtypeStruct(queries.shape, BF16),
            jax.ShapeDtypeStruct(joint_shape, BF16),
            jax.ShapeDtypeStruct((CHUNK, width), F32),
            jax.ShapeDtypeStruct((1, LATENT), F32),
        ),
        in_specs=[hbm_spec()] * 5,
        out_specs=(hbm_spec(),) * 4,
        scratch_shapes=[
            pltpu.VMEM((JOINT, SEQ), BF16),
            pltpu.VMEM((1, LATENT), F32),
            pltpu.VMEM(expand_weight.shape, BF16),
            pltpu.VMEM(queries.shape, BF16),
            pltpu.VMEM(grad_output.shape, BF16),
            sem((5,)),
            pltpu.VMEM(queries.shape, BF16),
            pltpu.VMEM(joint_shape, BF16),
            pltpu.VMEM((CHUNK, width), F32),
            pltpu.VMEM((1, LATENT), F32),
            sem((4,)),
            pltpu.VMEM((SEQ, LATENT), F32),
            pltpu.VMEM((SEQ, 128), F32),
            pltpu.VMEM((SEQ, LATENT), BF16),
            pltpu.VMEM((LATENT, SEQ), BF16),
            pltpu.VMEM((SEQ, 128), F32),
            pltpu.VMEM((SEQ, 128), F32),
            pltpu.VMEM((SEQ, width), BF16),
            pltpu.VMEM((SEQ, 256), BF16),
            pltpu.VMEM((SEQ, VALUE), BF16),
            pltpu.VMEM((SEQ, SEQ), BF16),
            pltpu.VMEM((SEQ, SEQ), BF16),
            pltpu.VMEM(joint_shape, BF16),
            pltpu.VMEM((8, 128), F32),
            pltpu.VMEM((16, 2, CHUNK, width), BF16),
            pltpu.VMEM((4, 4, CHUNK, PADDED), BF16),
            pltpu.VMEM((4, 4, CHUNK, PADDED), BF16),
            pltpu.VMEM((3, 4, CHUNK, PADDED), BF16),
            pltpu.VMEM((4, CHUNK, PADDED), BF16),
            pltpu.VMEM((3, CHUNK, PADDED), BF16),
            pltpu.VMEM((16, CHUNK, width), BF16),
            pltpu.VMEM((16, CHUNK, width), BF16),
            pltpu.VMEM((3, 4, CHUNK, width), BF16),
            pltpu.VMEM((4, CHUNK, width), BF16),
            pltpu.VMEM((3, CHUNK, width), BF16),
            pltpu.VMEM((2, 8, 128), F32),
            pltpu.VMEM((2, 8, 128), F32),
            pltpu.VMEM((4, 8, 128), F32),
            pltpu.VMEM((4, 8, 128), F32),
            pltpu.VMEM((4, 8, 128), F32),
            pltpu.VMEM((4, 8, 128), F32),
            sem((2, 4, 4)),
            sem((2, 3, 4)),
            sem((2, 3)),
            sem((2, 4)),
            sem((2, 3)),
            sem((2, 3)),
            sem((2, 3)),
            sem((2, 3, 4)),
            sem((2, 4, 4)),
            sem((2, 2)),
            sem((2, 4, 3)),
        ],
        compiler_params=pltpu.CompilerParams(
            collective_id=0, has_side_effects=True, vmem_limit_bytes=58 * 2**20
        ),
    )(
        latent_with_rope.T,
        latent_norm_weight.reshape(1, LATENT),
        expand_weight,
        queries,
        grad_output,
    )
    grad_queries, joint_t, grad_up_weight, gain = pl.pallas_call(
        write_body,
        name="write",
        out_shape=(
            jax.ShapeDtypeStruct(queries.shape, BF16),
            jax.ShapeDtypeStruct((JOINT, SEQ), BF16),
            jax.ShapeDtypeStruct((CHUNK, width), F32),
            jax.ShapeDtypeStruct((1, LATENT), F32),
        ),
        in_specs=[hbm_spec()] * 4,
        out_specs=(hbm_spec(),) * 4,
        scratch_shapes=[
            pltpu.VMEM(queries.shape, BF16),
            pltpu.VMEM(joint_shape, BF16),
            pltpu.VMEM((CHUNK, width), F32),
            pltpu.VMEM((1, LATENT), F32),
            pltpu.VMEM((JOINT, SEQ), BF16),
            sem((8,)),
        ],
        compiler_params=pltpu.CompilerParams(vmem_limit_bytes=58 * 2**20),
    )(grad_query, joint, up, gain)
    return grad_queries, joint_t.T, grad_up_weight, gain.reshape(LATENT)


def solution(mesh):
    assert mesh.shape["dp"] == NX * NY * NCORE and mesh.shape["tensor"] == NZ * NLO
    placed = (P("dp", None), P(), P(None, "tensor"), P("dp", "tensor"), P("dp", "tensor"))
    return jax.shard_map(
        per_device,
        mesh=mesh,
        in_specs=placed,
        out_specs=(P("dp", "tensor"), P("dp", None), P("dp", "tensor"), P()),
        check_vma=False,
    )
```

```python
import functools
import math

import jax
import jax.numpy as jnp
from jax import lax
from jax.experimental import pallas as pl
from jax.experimental.pallas import tpu as pltpu
from jax.sharding import PartitionSpec as P

ROPE = 64
NOPE = 128
VALUE = 128
LATENT = 512
JOINT = LATENT + ROPE
PADDED = LATENT + 128
SEQ = 512
HALF = SEQ // 2
CHUNK = 16
NX, NY, NCORE = 4, 4, 2
NZ, NLO = 16, 2

soft_scale = (1.0 + 0.1 * math.log(40.0)) ** 2 / math.sqrt(192.0)
exp2_scale = soft_scale * math.log2(math.e)
epsilon = 1e-06

F32 = jnp.float32
BF16 = jnp.bfloat16
MESH = pl.DeviceIdType.MESH


def dot(a, b, contract):
    return lax.dot_general(a, b, (contract, ((), ())), preferred_element_type=F32)


def head_probs(scores, grads):
    keep = lax.broadcasted_iota(jnp.int32, (HALF, HALF), 0) <= lax.broadcasted_iota(
        jnp.int32, (HALF, HALF), 1
    )
    scores = scores[:-1] + [jnp.where(keep, scores[-1], -jnp.inf)]
    top = functools.reduce(
        jnp.maximum, [jnp.max(block, axis=0, keepdims=True) for block in scores]
    )
    shift = top * exp2_scale
    weights = [jnp.exp2(block * exp2_scale - shift) for block in scores]
    total = sum(jnp.sum(block, axis=0, keepdims=True) for block in weights)
    inverse = 1.0 / total
    probs = [block * inverse for block in weights]
    delta = sum(
        jnp.sum(prob * grad, axis=0, keepdims=True) for prob, grad in zip(probs, grads)
    )
    grad_scores = [
        (prob * (grad - delta) * soft_scale).astype(BF16) for prob, grad in zip(probs, grads)
    ]
    return [prob.astype(BF16) for prob in probs], grad_scores


def transposed_rows(row):
    return jnp.broadcast_to(row, (128, row.shape[1])).T


def wide_columns(block):
    return jnp.concatenate([block] * (LATENT // 128), axis=1)


def attention_part(lat, weight, expand, query, grad_out, grad_query, joint_part, gain_part,
                   unit, inverse, normed, normed_t, rope_pad, rope_sum, grad_up, key_pad, value,
                   probs, grad_scores, loads):
    heads = expand.shape[1] // (NOPE + VALUE)
    loads[0].wait()
    loads[1].wait()
    state = lat[:LATENT, :].astype(F32)
    inverse_row = lax.rsqrt(jnp.mean(state * state, axis=0, keepdims=True) + epsilon)
    unit_t = state * inverse_row
    inverse[...] = transposed_rows(inverse_row)
    unit[...] = unit_t.T
    normed[...] = (unit[...] * weight[...]).astype(BF16)
    normed_t[...] = (unit_t * wide_columns(transposed_rows(weight[...]))).astype(BF16)
    rope_pad[...] = jnp.concatenate(
        [lat[LATENT:, :].astype(F32), jnp.zeros((128 - ROPE, SEQ), F32)], axis=0
    ).T
    rope_sum[...] = jnp.zeros_like(rope_sum)

    low, high, whole = slice(0, HALF), slice(HALF, SEQ), slice(0, SEQ)
    loads[2].wait()
    for head in range(heads):
        odd = head % 2
        columns = slice(head * 256, (head + 1) * 256)
        wide = slice((head // 2) * 384 + odd * 128, (head // 2) * 384 + odd * 128 + 256)
        own = slice(head * VALUE, (head + 1) * VALUE)
        projected = dot(normed[...], expand[:, columns], ((1,), (0,)))
        value[...] = projected[:, NOPE:].astype(BF16)
        keys = jnp.concatenate([projected[:, :NOPE], rope_pad[...]], axis=1)
        if odd:
            keys = pltpu.roll(keys, 64, 1)
        key_pad[...] = keys.astype(BF16)
        if head == 0:
            loads[3].wait()
            loads[4].wait()
        for rows, blocks in ((low, (low,)), (high, (low, high))):
            scores = [dot(key_pad[b, :], query[rows, wide], ((1,), (1,))) for b in blocks]
            grads = [dot(value[b, :], grad_out[rows, own], ((1,), (1,))) for b in blocks]
            prob, grad_score = head_probs(scores, grads)
            for b, p, g in zip(blocks, prob, grad_score):
                probs[b, rows] = p
                grad_scores[b, rows] = g
        out_low = dot(grad_scores[low, low], key_pad[low, :], ((0,), (0,)))
        out_high = dot(grad_scores[:, high], key_pad[...], ((0,), (0,)))
        base = (head // 2) * 384
        for rows, out in ((low, out_low), (high, out_high)):
            if odd:
                grad_query[rows, base + 128:base + 256] = (
                    grad_query[rows, base + 128:base + 256] + out[:, :128].astype(BF16)
                )
                grad_query[rows, base + 256:base + 384] = out[:, 128:].astype(BF16)
            else:
                grad_query[rows, base:base + 256] = out.astype(BF16)
        for rows, used in ((low, whole), (high, high)):
            grad_key = dot(grad_scores[rows, used], query[used, wide], ((1,), (0,)))
            grad_value = dot(probs[rows, used], grad_out[used, own], ((1,), (0,)))
            if odd:
                grad_key = pltpu.roll(grad_key, 192, 1)
            grad_up[rows, head * 256:head * 256 + NOPE] = grad_key[:, :NOPE].astype(BF16)
            grad_up[rows, head * 256 + NOPE:(head + 1) * 256] = grad_value.astype(BF16)
            rope_sum[rows, :] += grad_key[:, NOPE:]

    gain = jnp.zeros((1, LATENT), F32)
    for part in range(4):
        rows = slice(part * 128, (part + 1) * 128)
        grad_normed = dot(grad_up[rows, :], expand[...], ((1,), (1,)))
        gain = gain + jnp.sum(grad_normed * unit[rows, :], axis=0, keepdims=True)
        joint_part[part, :, :, :, :LATENT] = grad_normed.astype(BF16).reshape(
            2, 4, CHUNK, LATENT
        )
        joint_part[part, :, :, :, LATENT:] = rope_sum[rows, :].astype(BF16).reshape(
            2, 4, CHUNK, 128
        )
    gain_part[...] = jnp.zeros_like(gain_part)
    for piece in range(4):
        gain_part[piece:piece + 1, :] = gain[:, piece * 128:(piece + 1) * 128]


def up_gradient(normed_t, grad_up, up_part):
    for head in range(grad_up.shape[1] // 256):
        columns = slice(head * 256, (head + 1) * 256)
        up_part[:, :, :, columns] = (
            dot(normed_t[...], grad_up[:, columns], ((1,), (0,)))
            .astype(BF16)
            .reshape(16, 2, CHUNK, 256)
        )


def body(lat_hbm, weight_hbm, expand_hbm, query_hbm, grad_out_hbm,
         grad_query_hbm, joint_hbm, up_hbm, gain_hbm,
         lat, weight, expand, query, grad_out, load_sem, grad_query, joint, up, gain_out, save_sem,
         unit, inverse, normed, normed_t, rope_pad, rope_sum, grad_up, key_pad, value, probs,
         grad_scores, joint_part, gain_part, up_part,
         near_in, near_sum, far_in, core_in, core_sum, x_in, y_sum, y_in,
         gain_lo, gain_core, gain_far, gain_near, gain_x, gain_y,
         near_sem, far_sem, core_sem, x_sem, y_sem, out_far_sem, out_near_sem,
         gain_pair_sem, gain_quad_sem):
    d, t = lax.axis_index("dp"), lax.axis_index("tensor")
    core, y, x = d % 2, (d // 2) % 4, d // 8
    lo, z = t % 2, t // 2
    quarter, phase = z // 4, z % 4

    def z_plus(step, side=0):
        return (d, ((z + step + NZ) % NZ) * 2 + (1 - lo if side else lo))

    lo_peer = (d, t + 1 - 2 * lo)
    core_peer = (d + 1 - 2 * core, t)
    x_peers = [((((x + j) % 4) * 4 + y) * 2 + core, t) for j in (1, 2, 3)]
    y_peers = [((x * 4 + (y + j) % 4) * 2 + core, t) for j in (1, 2, 3)]
    far_peers = [z_plus(4 * j) for j in (1, 2, 3)]
    near_peers = {(s, side): z_plus(s, side) for s in (1, -1, 2, -2) for side in (0, 1)}
    near_peers[0, 1] = lo_peer

    barrier = pltpu.get_barrier_semaphore()
    peers = far_peers + [core_peer] + x_peers + y_peers + list(near_peers.values())
    for peer in peers:
        pl.semaphore_signal(barrier, inc=1, device_id=peer, device_id_type=MESH)

    loads = []
    for i, (src, dst) in enumerate(
        ((lat_hbm, lat), (weight_hbm, weight), (expand_hbm, expand), (query_hbm, query),
         (grad_out_hbm, grad_out))
    ):
        loads.append(pltpu.make_async_copy(src, dst, load_sem.at[i]))
        loads[-1].start()

    attention_part(lat, weight, expand, query, grad_out, grad_query, joint_part, gain_part,
                   unit, inverse, normed, normed_t, rope_pad, rope_sum, grad_up, key_pad, value,
                   probs, grad_scores, loads)
    saves = [pltpu.make_async_copy(grad_query, grad_query_hbm, save_sem.at[0])]
    saves[0].start()

    pl.semaphore_wait(barrier, len(peers))

    started = []

    def send(src, dst, sems, slot, recv_slot, peer):
        copy = pltpu.make_async_remote_copy(
            src_ref=src, dst_ref=dst, send_sem=sems.at[(0,) + slot],
            recv_sem=sems.at[(1,) + recv_slot], device_id=peer, device_id_type=MESH,
        )
        copy.start()
        started.append(copy)

    def arrive(dst, sems, recv_slot, peer):
        pltpu.make_async_remote_copy(
            src_ref=dst, dst_ref=dst, send_sem=sems.at[(0,) + recv_slot],
            recv_sem=sems.at[(1,) + recv_slot], device_id=peer, device_id_type=MESH,
        ).wait_recv()

    def gain_pair_send(value, slots, index, me, peer):
        slots[me] = value
        send(slots.at[me], slots.at[me], gain_pair_sem, (index,), (index,), peer)

    def gain_pair_sum(slots, index, me, peer):
        arrive(slots.at[1 - me], gain_pair_sem, (index,), peer)
        return slots[0] + slots[1]

    def gain_quad_send(value, slots, index, me, peers_of):
        slots[me] = value
        for j, peer in enumerate(peers_of):
            send(slots.at[me], slots.at[me], gain_quad_sem, (index, j), (index, j), peer)

    def gain_quad_sum(slots, index, me, steps, peers_of):
        for j, (step, peer) in enumerate(zip(steps, peers_of)):
            arrive(slots.at[(me + (4 - step)) % 4], gain_quad_sem, (index, j), peer)
        return (slots[0] + slots[1]) + (slots[2] + slots[3])

    order = (2, 1, 3, 0)
    slot_of = {(1, 0): 0, (-1, 0): 1, (2, 0): 2, (0, 1): 3, (1, 1): 4, (-1, 1): 5, (2, 1): 6}

    def collected(step, delta):
        holder = quarter if delta in (0, 2) else ((z + delta + NZ) % NZ) // 4
        return (holder + step) % 4, (phase + delta + 4) % 4

    def near_peer(delta, side, a):
        return z_plus(2 - 4 * (a // 2), side) if delta == 2 else near_peers[delta, side]

    gain_pair_send(gain_part[...], gain_lo, 0, lo, lo_peer)
    for step in order:
        for (delta, side), slot in reversed(slot_of.items()):
            a, k = collected(step, delta)
            send(joint_part.at[a, 1 - lo if side else lo, k], near_in.at[slot, a], near_sem,
                 (slot, a), (slot, a), near_peer(delta, side, a))

    up_gradient(normed_t, grad_up, up_part)
    for i in range(4):
        send(up_part.at[pl.ds(4 * i, 4), 1 - core], core_in.at[pl.ds(4 * i, 4)], core_sem,
             (i,), (i,), core_peer)

    def near_step(step):
        a = (quarter + step) % 4
        for (delta, side), slot in slot_of.items():
            arrive(near_in.at[slot, a], near_sem, (slot, a), near_peers[-delta, side])
        near_sum[a] = (
            (
                (joint_part[a, lo, phase].astype(F32) + near_in[0, a].astype(F32))
                + (near_in[1, a].astype(F32) + near_in[2, a].astype(F32))
            )
            + (
                (near_in[3, a].astype(F32) + near_in[4, a].astype(F32))
                + (near_in[5, a].astype(F32) + near_in[6, a].astype(F32))
            )
        ).astype(BF16)
        if step:
            send(near_sum.at[a], far_in.at[step - 1], far_sem, (step - 1,), (step - 1,),
                 far_peers[step - 1])

    gain_value = gain_pair_sum(gain_lo, 0, lo, lo_peer)
    gain_pair_send(gain_value, gain_core, 1, core, core_peer)
    gain_value = gain_pair_sum(gain_core, 1, core, core_peer)
    gain_quad_send(gain_value, gain_far, 0, quarter, far_peers)

    for i in range(4):
        arrive(core_in.at[pl.ds(4 * i, 4)], core_sem, (i,), core_peer)
    for j in (2, 1, 3, 0):
        rows = pl.ds(((x + j) % 4) * 4, 4)
        core_sum[rows] = (
            up_part[rows, core].astype(F32) + core_in[rows].astype(F32)
        ).astype(BF16)
        if j:
            send(core_sum.at[rows], x_in.at[j - 1], x_sem, (j - 1,), (j - 1,), x_peers[j - 1])

    for step in order:
        near_step(step)
    gain_value = gain_quad_sum(gain_far, 0, quarter, (1, 2, 3), far_peers[::-1])
    gain_near_peers = [near_peers[1, 0], near_peers[-1, 0], near_peers[2, 0]]
    gain_quad_send(gain_value, gain_near, 1, phase, gain_near_peers)

    first = pl.multiple_of(quarter * 128 + lo * 64 + phase * CHUNK, CHUNK)
    own_unit = unit[pl.ds(first, CHUNK), :]
    own_inverse = wide_columns(inverse[pl.ds(first, CHUNK), :])
    for j in (1, 3, 2):
        arrive(far_in.at[j - 1], far_sem, (j - 1,), far_peers[3 - j])
    total = (near_sum[quarter].astype(F32) + far_in[0].astype(F32)) + (
        far_in[1].astype(F32) + far_in[2].astype(F32)
    )
    scaled = total[:, :LATENT] * weight[...]
    grad_latent = own_inverse * (
        scaled - own_unit * jnp.mean(scaled * own_unit, axis=1, keepdims=True)
    )
    joint[quarter, lo, phase, :, :LATENT] = grad_latent.astype(BF16)
    joint[quarter, lo, phase, :, LATENT:] = total[:, LATENT:].astype(BF16)

    def spread(step):
        a = (quarter + 4 - step) % 4
        chunk = joint.at[a, lo, phase]
        if step:
            arrive(chunk, out_far_sem, (step - 1,), far_peers[3 - step])
        else:
            for j in (2, 1, 3):
                send(chunk, chunk, out_far_sem, (j - 1,), (j - 1,), far_peers[j - 1])
        for (delta, side), slot in reversed(slot_of.items()):
            send(chunk, chunk, out_near_sem, (slot, a), (slot, a), near_peer(delta, side, a))

    spread(0)
    gain_value = gain_quad_sum(
        gain_near, 1, phase, (1, 3, 2), [near_peers[-1, 0], near_peers[1, 0], near_peers[-2, 0]]
    )
    gain_quad_send(gain_value, gain_x, 2, x, x_peers)
    for j in (1, 3, 2):
        arrive(x_in.at[j - 1], x_sem, (j - 1,), x_peers[3 - j])
    y_sum[...] = (
        (core_sum[pl.ds(x * 4, 4)].astype(F32) + x_in[0].astype(F32))
        + (x_in[1].astype(F32) + x_in[2].astype(F32))
    ).astype(BF16)
    for j in (2, 1, 3):
        send(y_sum.at[(y + j) % 4], y_in.at[j - 1], y_sem, (j - 1,), (j - 1,), y_peers[j - 1])
    gain_value = gain_quad_sum(gain_x, 2, x, (1, 2, 3), x_peers[::-1])
    gain_quad_send(gain_value, gain_y, 3, y, y_peers)
    spread(1)
    spread(3)
    spread(2)
    for j in (1, 3, 2):
        arrive(y_in.at[j - 1], y_sem, (j - 1,), y_peers[3 - j])
    up[...] = (y_sum[y].astype(F32) + y_in[0].astype(F32)) + (
        y_in[1].astype(F32) + y_in[2].astype(F32)
    )
    saves.append(pltpu.make_async_copy(up, up_hbm, save_sem.at[1]))
    saves[-1].start()
    gain_value = gain_quad_sum(gain_y, 3, y, (1, 2, 3), y_peers[::-1])
    for piece in range(4):
        gain_out[:, piece * 128:(piece + 1) * 128] = gain_value[piece:piece + 1, :]
    saves.append(pltpu.make_async_copy(gain_out, gain_hbm, save_sem.at[2]))
    saves[-1].start()
    for (delta, side), slot in slot_of.items():
        for a in range(4):
            chunk = joint.at[a, 1 - lo if side else lo, (phase - delta + 4) % 4]
            arrive(chunk, out_near_sem, (slot, a), near_peers[-delta, side])
    saves.append(pltpu.make_async_copy(joint, joint_hbm, save_sem.at[3]))
    saves[-1].start()
    for copy in started:
        copy.wait_send()
    for save in saves:
        save.wait()


def write_body(grad_query_in, joint_in, up_in, gain_in, grad_query_out, joint_out, up_out, gain_out,
               grad_query, joint, up, gain, joint_t, sems):
    def copies(pairs, first):
        return [
            pltpu.make_async_copy(src, dst, sems.at[first + i]) for i, (src, dst) in enumerate(pairs)
        ]

    reads = copies(
        ((joint_in, joint), (grad_query_in, grad_query), (up_in, up), (gain_in, gain)), 0
    )
    writes = copies(
        ((joint_t, joint_out), (grad_query, grad_query_out), (up, up_out), (gain, gain_out)), 4
    )
    for copy in reads:
        copy.start()
    reads[0].wait()
    for part in range(4):
        rows = joint[part].reshape(128, PADDED)
        joint_t[:, part * 128:(part + 1) * 128] = rows.astype(F32).T[:JOINT, :].astype(BF16)
    writes[0].start()
    for read, write in zip(reads[1:], writes[1:]):
        read.wait()
        write.start()
    for copy in writes:
        copy.wait()


def hbm_spec():
    return pl.BlockSpec(memory_space=pltpu.HBM)


def per_device(latent_with_rope, latent_norm_weight, expand_weight, queries, grad_output):
    width = expand_weight.shape[1]
    sem = pltpu.SemaphoreType.DMA
    joint_shape = (4, 2, 4, CHUNK, PADDED)
    grad_query, joint, up, gain = pl.pallas_call(
        body,
        name="attention_and_sums",
        out_shape=(
            jax.ShapeDtypeStruct(queries.shape, BF16),
            jax.ShapeDtypeStruct(joint_shape, BF16),
            jax.ShapeDtypeStruct((CHUNK, width), F32),
            jax.ShapeDtypeStruct((1, LATENT), F32),
        ),
        in_specs=[hbm_spec()] * 5,
        out_specs=(hbm_spec(),) * 4,
        scratch_shapes=[
            pltpu.VMEM((JOINT, SEQ), BF16),
            pltpu.VMEM((1, LATENT), F32),
            pltpu.VMEM(expand_weight.shape, BF16),
            pltpu.VMEM(queries.shape, BF16),
            pltpu.VMEM(grad_output.shape, BF16),
            sem((5,)),
            pltpu.VMEM(queries.shape, BF16),
            pltpu.VMEM(joint_shape, BF16),
            pltpu.VMEM((CHUNK, width), F32),
            pltpu.VMEM((1, LATENT), F32),
            sem((4,)),
            pltpu.VMEM((SEQ, LATENT), F32),
            pltpu.VMEM((SEQ, 128), F32),
            pltpu.VMEM((SEQ, LATENT), BF16),
            pltpu.VMEM((LATENT, SEQ), BF16),
            pltpu.VMEM((SEQ, 128), F32),
            pltpu.VMEM((SEQ, 128), F32),
            pltpu.VMEM((SEQ, width), BF16),
            pltpu.VMEM((SEQ, 256), BF16),
            pltpu.VMEM((SEQ, VALUE), BF16),
            pltpu.VMEM((SEQ, SEQ), BF16),
            pltpu.VMEM((SEQ, SEQ), BF16),
            pltpu.VMEM(joint_shape, BF16),
            pltpu.VMEM((8, 128), F32),
            pltpu.VMEM((16, 2, CHUNK, width), BF16),
            pltpu.VMEM((7, 4, CHUNK, PADDED), BF16),
            pltpu.VMEM((4, CHUNK, PADDED), BF16),
            pltpu.VMEM((3, CHUNK, PADDED), BF16),
            pltpu.VMEM((16, CHUNK, width), BF16),
            pltpu.VMEM((16, CHUNK, width), BF16),
            pltpu.VMEM((3, 4, CHUNK, width), BF16),
            pltpu.VMEM((4, CHUNK, width), BF16),
            pltpu.VMEM((3, CHUNK, width), BF16),
            pltpu.VMEM((2, 8, 128), F32),
            pltpu.VMEM((2, 8, 128), F32),
            pltpu.VMEM((4, 8, 128), F32),
            pltpu.VMEM((4, 8, 128), F32),
            pltpu.VMEM((4, 8, 128), F32),
            pltpu.VMEM((4, 8, 128), F32),
            sem((2, 7, 4)),
            sem((2, 3)),
            sem((2, 4)),
            sem((2, 3)),
            sem((2, 3)),
            sem((2, 3)),
            sem((2, 7, 4)),
            sem((2, 2)),
            sem((2, 4, 3)),
        ],
        compiler_params=pltpu.CompilerParams(
            collective_id=0, has_side_effects=True, vmem_limit_bytes=58 * 2**20
        ),
    )(
        latent_with_rope.T,
        latent_norm_weight.reshape(1, LATENT),
        expand_weight,
        queries,
        grad_output,
    )
    grad_queries, joint_t, grad_up_weight, gain = pl.pallas_call(
        write_body,
        name="write",
        out_shape=(
            jax.ShapeDtypeStruct(queries.shape, BF16),
            jax.ShapeDtypeStruct((JOINT, SEQ), BF16),
            jax.ShapeDtypeStruct((CHUNK, width), F32),
            jax.ShapeDtypeStruct((1, LATENT), F32),
        ),
        in_specs=[hbm_spec()] * 4,
        out_specs=(hbm_spec(),) * 4,
        scratch_shapes=[
            pltpu.VMEM(queries.shape, BF16),
            pltpu.VMEM(joint_shape, BF16),
            pltpu.VMEM((CHUNK, width), F32),
            pltpu.VMEM((1, LATENT), F32),
            pltpu.VMEM((JOINT, SEQ), BF16),
            sem((8,)),
        ],
        compiler_params=pltpu.CompilerParams(vmem_limit_bytes=58 * 2**20),
    )(grad_query, joint, up, gain)
    return grad_queries, joint_t.T, grad_up_weight, gain.reshape(LATENT)


def solution(mesh):
    assert mesh.shape["dp"] == NX * NY * NCORE and mesh.shape["tensor"] == NZ * NLO
    placed = (P("dp", None), P(), P(None, "tensor"), P("dp", "tensor"), P("dp", "tensor"))
    return jax.shard_map(
        per_device,
        mesh=mesh,
        in_specs=placed,
        out_specs=(P("dp", "tensor"), P("dp", None), P("dp", "tensor"), P()),
        check_vma=False,
    )
```

```python
import functools
import math

import jax
import jax.numpy as jnp
from jax import lax
from jax.experimental import pallas as pl
from jax.experimental.pallas import tpu as pltpu
from jax.sharding import PartitionSpec as P

ROPE = 64
NOPE = 128
VALUE = 128
LATENT = 512
JOINT = LATENT + ROPE
PADDED = LATENT + ROPE
SEQ = 512
HALF = SEQ // 2
CHUNK = 16
NX, NY, NCORE = 4, 4, 2
NZ, NLO = 16, 2

soft_scale = (1.0 + 0.1 * math.log(40.0)) ** 2 / math.sqrt(192.0)
exp2_scale = soft_scale * math.log2(math.e)
epsilon = 1e-06

F32 = jnp.float32
BF16 = jnp.bfloat16
MESH = pl.DeviceIdType.MESH


def dot(a, b, contract):
    return lax.dot_general(a, b, (contract, ((), ())), preferred_element_type=F32)


def head_probs(scores, grads):
    keep = lax.broadcasted_iota(jnp.int32, (HALF, HALF), 0) <= lax.broadcasted_iota(
        jnp.int32, (HALF, HALF), 1
    )
    scores = scores[:-1] + [jnp.where(keep, scores[-1], -jnp.inf)]
    top = functools.reduce(
        jnp.maximum, [jnp.max(block, axis=0, keepdims=True) for block in scores]
    )
    shift = top * exp2_scale
    weights = [jnp.exp2(block * exp2_scale - shift) for block in scores]
    total = sum(jnp.sum(block, axis=0, keepdims=True) for block in weights)
    inverse = 1.0 / total
    probs = [block * inverse for block in weights]
    delta = sum(
        jnp.sum(prob * grad, axis=0, keepdims=True) for prob, grad in zip(probs, grads)
    )
    grad_scores = [
        (prob * (grad - delta) * soft_scale).astype(BF16) for prob, grad in zip(probs, grads)
    ]
    return [prob.astype(BF16) for prob in probs], grad_scores


def transposed_rows(row):
    return jnp.broadcast_to(row, (128, row.shape[1])).T


def wide_columns(block):
    return jnp.concatenate([block] * (LATENT // 128), axis=1)


def attention_part(lat, weight, expand, query, grad_out, grad_query, joint_part, gain_part,
                   unit, inverse, normed, normed_t, rope_pad, rope_sum, grad_up, key_pad, value,
                   probs, grad_scores, loads):
    heads = expand.shape[1] // (NOPE + VALUE)
    loads[0].wait()
    loads[1].wait()
    state = lat[:LATENT, :].astype(F32)
    inverse_row = lax.rsqrt(jnp.mean(state * state, axis=0, keepdims=True) + epsilon)
    unit_t = state * inverse_row
    inverse[...] = transposed_rows(inverse_row)
    unit[...] = unit_t.T
    normed[...] = (unit[...] * weight[...]).astype(BF16)
    normed_t[...] = (unit_t * wide_columns(transposed_rows(weight[...]))).astype(BF16)
    rope_pad[...] = jnp.concatenate(
        [lat[LATENT:, :].astype(F32), jnp.zeros((128 - ROPE, SEQ), F32)], axis=0
    ).T
    rope_sum[...] = jnp.zeros_like(rope_sum)

    low, high, whole = slice(0, HALF), slice(HALF, SEQ), slice(0, SEQ)
    loads[2].wait()
    for head in range(heads):
        odd = head % 2
        columns = slice(head * 256, (head + 1) * 256)
        wide = slice((head // 2) * 384 + odd * 128, (head // 2) * 384 + odd * 128 + 256)
        own = slice(head * VALUE, (head + 1) * VALUE)
        projected = dot(normed[...], expand[:, columns], ((1,), (0,)))
        value[...] = projected[:, NOPE:].astype(BF16)
        keys = jnp.concatenate([projected[:, :NOPE], rope_pad[...]], axis=1)
        if odd:
            keys = pltpu.roll(keys, 64, 1)
        key_pad[...] = keys.astype(BF16)
        if head == 0:
            loads[3].wait()
            loads[4].wait()
        for rows, blocks in ((low, (low,)), (high, (low, high))):
            scores = [dot(key_pad[b, :], query[rows, wide], ((1,), (1,))) for b in blocks]
            grads = [dot(value[b, :], grad_out[rows, own], ((1,), (1,))) for b in blocks]
            prob, grad_score = head_probs(scores, grads)
            for b, p, g in zip(blocks, prob, grad_score):
                probs[b, rows] = p
                grad_scores[b, rows] = g
        out_low = dot(grad_scores[low, low], key_pad[low, :], ((0,), (0,)))
        out_high = dot(grad_scores[:, high], key_pad[...], ((0,), (0,)))
        base = (head // 2) * 384
        for rows, out in ((low, out_low), (high, out_high)):
            if odd:
                grad_query[rows, base + 128:base + 256] = (
                    grad_query[rows, base + 128:base + 256] + out[:, :128].astype(BF16)
                )
                grad_query[rows, base + 256:base + 384] = out[:, 128:].astype(BF16)
            else:
                grad_query[rows, base:base + 256] = out.astype(BF16)
        for rows, used in ((low, whole), (high, high)):
            grad_key = dot(grad_scores[rows, used], query[used, wide], ((1,), (0,)))
            grad_value = dot(probs[rows, used], grad_out[used, own], ((1,), (0,)))
            if odd:
                grad_key = pltpu.roll(grad_key, 192, 1)
            grad_up[rows, head * 256:head * 256 + NOPE] = grad_key[:, :NOPE].astype(BF16)
            grad_up[rows, head * 256 + NOPE:(head + 1) * 256] = grad_value.astype(BF16)
            rope_sum[rows, :] += grad_key[:, NOPE:]

    gain = jnp.zeros((1, LATENT), F32)
    for part in range(4):
        rows = slice(part * 128, (part + 1) * 128)
        grad_normed = dot(grad_up[rows, :], expand[...], ((1,), (1,)))
        gain = gain + jnp.sum(grad_normed * unit[rows, :], axis=0, keepdims=True)
        joint_part[part, :, :, :, :LATENT] = grad_normed.astype(BF16).reshape(
            2, 4, CHUNK, LATENT
        )
        joint_part[part, :, :, :, LATENT:] = rope_sum[rows, :ROPE].astype(BF16).reshape(
            2, 4, CHUNK, ROPE
        )
    gain_part[...] = jnp.zeros_like(gain_part)
    for piece in range(4):
        gain_part[piece:piece + 1, :] = gain[:, piece * 128:(piece + 1) * 128]


def up_gradient(normed_t, grad_up, up_part):
    for head in range(grad_up.shape[1] // 256):
        columns = slice(head * 256, (head + 1) * 256)
        up_part[:, :, :, columns] = (
            dot(normed_t[...], grad_up[:, columns], ((1,), (0,)))
            .astype(BF16)
            .reshape(16, 2, CHUNK, 256)
        )


def body(lat_hbm, weight_hbm, expand_hbm, query_hbm, grad_out_hbm,
         grad_query_hbm, joint_hbm, up_hbm, gain_hbm,
         lat, weight, expand, query, grad_out, load_sem, grad_query, joint, up, gain_out, save_sem,
         unit, inverse, normed, normed_t, rope_pad, rope_sum, grad_up, key_pad, value, probs,
         grad_scores, joint_part, gain_part, up_part,
         near_in, near_sum, far_in, core_in, core_sum, x_in, y_sum, y_in,
         gain_lo, gain_core, gain_far, gain_near, gain_x, gain_y,
         near_sem, far_sem, core_sem, x_sem, y_sem, out_far_sem, out_near_sem,
         gain_pair_sem, gain_quad_sem):
    d, t = lax.axis_index("dp"), lax.axis_index("tensor")
    core, y, x = d % 2, (d // 2) % 4, d // 8
    lo, z = t % 2, t // 2
    quarter, phase = z // 4, z % 4

    def z_plus(step, side=0):
        return (d, ((z + step + NZ) % NZ) * 2 + (1 - lo if side else lo))

    lo_peer = (d, t + 1 - 2 * lo)
    core_peer = (d + 1 - 2 * core, t)
    x_peers = [((((x + j) % 4) * 4 + y) * 2 + core, t) for j in (1, 2, 3)]
    y_peers = [((x * 4 + (y + j) % 4) * 2 + core, t) for j in (1, 2, 3)]
    far_peers = [z_plus(4 * j) for j in (1, 2, 3)]
    near_peers = {(s, side): z_plus(s, side) for s in (1, -1, 2, -2) for side in (0, 1)}
    near_peers[0, 1] = lo_peer

    barrier = pltpu.get_barrier_semaphore()
    peers = far_peers + [core_peer] + x_peers + y_peers + list(near_peers.values())
    for peer in peers:
        pl.semaphore_signal(barrier, inc=1, device_id=peer, device_id_type=MESH)

    loads = []
    for i, (src, dst) in enumerate(
        ((lat_hbm, lat), (weight_hbm, weight), (expand_hbm, expand), (query_hbm, query),
         (grad_out_hbm, grad_out))
    ):
        loads.append(pltpu.make_async_copy(src, dst, load_sem.at[i]))
        loads[-1].start()

    attention_part(lat, weight, expand, query, grad_out, grad_query, joint_part, gain_part,
                   unit, inverse, normed, normed_t, rope_pad, rope_sum, grad_up, key_pad, value,
                   probs, grad_scores, loads)
    saves = [pltpu.make_async_copy(grad_query, grad_query_hbm, save_sem.at[0])]
    saves[0].start()

    pl.semaphore_wait(barrier, len(peers))

    started = []

    def send(src, dst, sems, slot, recv_slot, peer):
        copy = pltpu.make_async_remote_copy(
            src_ref=src, dst_ref=dst, send_sem=sems.at[(0,) + slot],
            recv_sem=sems.at[(1,) + recv_slot], device_id=peer, device_id_type=MESH,
        )
        copy.start()
        started.append(copy)

    def arrive(dst, sems, recv_slot, peer):
        pltpu.make_async_remote_copy(
            src_ref=dst, dst_ref=dst, send_sem=sems.at[(0,) + recv_slot],
            recv_sem=sems.at[(1,) + recv_slot], device_id=peer, device_id_type=MESH,
        ).wait_recv()

    def gain_pair_send(value, slots, index, me, peer):
        slots[me] = value
        send(slots.at[me], slots.at[me], gain_pair_sem, (index,), (index,), peer)

    def gain_pair_sum(slots, index, me, peer):
        arrive(slots.at[1 - me], gain_pair_sem, (index,), peer)
        return slots[0] + slots[1]

    def gain_quad_send(value, slots, index, me, peers_of):
        slots[me] = value
        for j, peer in enumerate(peers_of):
            send(slots.at[me], slots.at[me], gain_quad_sem, (index, j), (index, j), peer)

    def gain_quad_sum(slots, index, me, steps, peers_of):
        for j, (step, peer) in enumerate(zip(steps, peers_of)):
            arrive(slots.at[(me + (4 - step)) % 4], gain_quad_sem, (index, j), peer)
        return (slots[0] + slots[1]) + (slots[2] + slots[3])

    order = (2, 1, 3, 0)
    slot_of = {(1, 0): 0, (-1, 0): 1, (2, 0): 2, (0, 1): 3, (1, 1): 4, (-1, 1): 5, (2, 1): 6}

    def collected(step, delta):
        holder = quarter if delta in (0, 2) else ((z + delta + NZ) % NZ) // 4
        return (holder + step) % 4, (phase + delta + 4) % 4

    def near_peer(delta, side, a):
        return z_plus(2 - 4 * (a // 2), side) if delta == 2 else near_peers[delta, side]

    gain_pair_send(gain_part[...], gain_lo, 0, lo, lo_peer)
    for step in order:
        for (delta, side), slot in reversed(slot_of.items()):
            a, k = collected(step, delta)
            send(joint_part.at[a, 1 - lo if side else lo, k], near_in.at[slot, a], near_sem,
                 (slot, a), (slot, a), near_peer(delta, side, a))

    up_gradient(normed_t, grad_up, up_part)
    for i in range(4):
        send(up_part.at[pl.ds(4 * i, 4), 1 - core], core_in.at[pl.ds(4 * i, 4)], core_sem,
             (i,), (i,), core_peer)

    def near_step(step):
        a = (quarter + step) % 4
        for (delta, side), slot in slot_of.items():
            arrive(near_in.at[slot, a], near_sem, (slot, a), near_peers[-delta, side])
        near_sum[a] = (
            (
                (joint_part[a, lo, phase].astype(F32) + near_in[0, a].astype(F32))
                + (near_in[1, a].astype(F32) + near_in[2, a].astype(F32))
            )
            + (
                (near_in[3, a].astype(F32) + near_in[4, a].astype(F32))
                + (near_in[5, a].astype(F32) + near_in[6, a].astype(F32))
            )
        ).astype(BF16)
        if step:
            send(near_sum.at[a], far_in.at[step - 1], far_sem, (step - 1,), (step - 1,),
                 far_peers[step - 1])

    gain_value = gain_pair_sum(gain_lo, 0, lo, lo_peer)
    gain_pair_send(gain_value, gain_core, 1, core, core_peer)
    gain_value = gain_pair_sum(gain_core, 1, core, core_peer)
    gain_quad_send(gain_value, gain_far, 0, quarter, far_peers)

    for i in range(4):
        arrive(core_in.at[pl.ds(4 * i, 4)], core_sem, (i,), core_peer)
    for j in (2, 1, 3, 0):
        rows = pl.ds(((x + j) % 4) * 4, 4)
        core_sum[rows] = (
            up_part[rows, core].astype(F32) + core_in[rows].astype(F32)
        ).astype(BF16)
        if j:
            send(core_sum.at[rows], x_in.at[j - 1], x_sem, (j - 1,), (j - 1,), x_peers[j - 1])

    for step in order:
        near_step(step)
    gain_value = gain_quad_sum(gain_far, 0, quarter, (1, 2, 3), far_peers[::-1])
    gain_near_peers = [near_peers[1, 0], near_peers[-1, 0], near_peers[2, 0]]
    gain_quad_send(gain_value, gain_near, 1, phase, gain_near_peers)

    first = pl.multiple_of(quarter * 128 + lo * 64 + phase * CHUNK, CHUNK)
    own_unit = unit[pl.ds(first, CHUNK), :]
    own_inverse = wide_columns(inverse[pl.ds(first, CHUNK), :])
    for j in (1, 3, 2):
        arrive(far_in.at[j - 1], far_sem, (j - 1,), far_peers[3 - j])
    total = (near_sum[quarter].astype(F32) + far_in[0].astype(F32)) + (
        far_in[1].astype(F32) + far_in[2].astype(F32)
    )
    scaled = total[:, :LATENT] * weight[...]
    grad_latent = own_inverse * (
        scaled - own_unit * jnp.mean(scaled * own_unit, axis=1, keepdims=True)
    )
    joint[quarter, lo, phase, :, :LATENT] = grad_latent.astype(BF16)
    joint[quarter, lo, phase, :, LATENT:] = total[:, LATENT:].astype(BF16)

    def spread(step):
        a = (quarter + 4 - step) % 4
        chunk = joint.at[a, lo, phase]
        if step:
            arrive(chunk, out_far_sem, (step - 1,), far_peers[3 - step])
        else:
            for j in (2, 1, 3):
                send(chunk, chunk, out_far_sem, (j - 1,), (j - 1,), far_peers[j - 1])
        for (delta, side), slot in reversed(slot_of.items()):
            send(chunk, chunk, out_near_sem, (slot, a), (slot, a), near_peer(delta, side, a))

    spread(0)
    gain_value = gain_quad_sum(
        gain_near, 1, phase, (1, 3, 2), [near_peers[-1, 0], near_peers[1, 0], near_peers[-2, 0]]
    )
    gain_quad_send(gain_value, gain_x, 2, x, x_peers)
    for j in (1, 3, 2):
        arrive(x_in.at[j - 1], x_sem, (j - 1,), x_peers[3 - j])
    y_sum[...] = (
        (core_sum[pl.ds(x * 4, 4)].astype(F32) + x_in[0].astype(F32))
        + (x_in[1].astype(F32) + x_in[2].astype(F32))
    ).astype(BF16)
    for j in (2, 1, 3):
        send(y_sum.at[(y + j) % 4], y_in.at[j - 1], y_sem, (j - 1,), (j - 1,), y_peers[j - 1])
    spread(1)
    spread(3)
    gain_value = gain_quad_sum(gain_x, 2, x, (1, 2, 3), x_peers[::-1])
    gain_quad_send(gain_value, gain_y, 3, y, y_peers)
    spread(2)
    for j in (1, 3, 2):
        arrive(y_in.at[j - 1], y_sem, (j - 1,), y_peers[3 - j])
    up[...] = (y_sum[y].astype(F32) + y_in[0].astype(F32)) + (
        y_in[1].astype(F32) + y_in[2].astype(F32)
    )
    saves.append(pltpu.make_async_copy(up, up_hbm, save_sem.at[1]))
    saves[-1].start()
    gain_value = gain_quad_sum(gain_y, 3, y, (1, 2, 3), y_peers[::-1])
    for piece in range(4):
        gain_out[:, piece * 128:(piece + 1) * 128] = gain_value[piece:piece + 1, :]
    saves.append(pltpu.make_async_copy(gain_out, gain_hbm, save_sem.at[2]))
    saves[-1].start()
    for (delta, side), slot in slot_of.items():
        for a in range(4):
            chunk = joint.at[a, 1 - lo if side else lo, (phase - delta + 4) % 4]
            arrive(chunk, out_near_sem, (slot, a), near_peers[-delta, side])
    saves.append(pltpu.make_async_copy(joint, joint_hbm, save_sem.at[3]))
    saves[-1].start()
    for copy in started:
        copy.wait_send()
    for save in saves:
        save.wait()


def write_body(grad_query_in, joint_in, up_in, gain_in, grad_query_out, joint_out, up_out, gain_out,
               grad_query, joint, up, gain, joint_t, sems):
    def copies(pairs, first):
        return [
            pltpu.make_async_copy(src, dst, sems.at[first + i]) for i, (src, dst) in enumerate(pairs)
        ]

    reads = copies(
        ((joint_in, joint), (grad_query_in, grad_query), (up_in, up), (gain_in, gain)), 0
    )
    writes = copies(
        ((joint_t, joint_out), (grad_query, grad_query_out), (up, up_out), (gain, gain_out)), 4
    )
    for copy in reads:
        copy.start()
    reads[0].wait()
    for part in range(4):
        rows = joint[part].reshape(128, PADDED)
        joint_t[:, part * 128:(part + 1) * 128] = rows.astype(F32).T[:JOINT, :].astype(BF16)
    writes[0].start()
    for read, write in zip(reads[1:], writes[1:]):
        read.wait()
        write.start()
    for copy in writes:
        copy.wait()


def hbm_spec():
    return pl.BlockSpec(memory_space=pltpu.HBM)


def per_device(latent_with_rope, latent_norm_weight, expand_weight, queries, grad_output):
    width = expand_weight.shape[1]
    sem = pltpu.SemaphoreType.DMA
    joint_shape = (4, 2, 4, CHUNK, PADDED)
    grad_query, joint, up, gain = pl.pallas_call(
        body,
        name="attention_and_sums",
        out_shape=(
            jax.ShapeDtypeStruct(queries.shape, BF16),
            jax.ShapeDtypeStruct(joint_shape, BF16),
            jax.ShapeDtypeStruct((CHUNK, width), F32),
            jax.ShapeDtypeStruct((1, LATENT), F32),
        ),
        in_specs=[hbm_spec()] * 5,
        out_specs=(hbm_spec(),) * 4,
        scratch_shapes=[
            pltpu.VMEM((JOINT, SEQ), BF16),
            pltpu.VMEM((1, LATENT), F32),
            pltpu.VMEM(expand_weight.shape, BF16),
            pltpu.VMEM(queries.shape, BF16),
            pltpu.VMEM(grad_output.shape, BF16),
            sem((5,)),
            pltpu.VMEM(queries.shape, BF16),
            pltpu.VMEM(joint_shape, BF16),
            pltpu.VMEM((CHUNK, width), F32),
            pltpu.VMEM((1, LATENT), F32),
            sem((4,)),
            pltpu.VMEM((SEQ, LATENT), F32),
            pltpu.VMEM((SEQ, 128), F32),
            pltpu.VMEM((SEQ, LATENT), BF16),
            pltpu.VMEM((LATENT, SEQ), BF16),
            pltpu.VMEM((SEQ, 128), F32),
            pltpu.VMEM((SEQ, 128), F32),
            pltpu.VMEM((SEQ, width), BF16),
            pltpu.VMEM((SEQ, 256), BF16),
            pltpu.VMEM((SEQ, VALUE), BF16),
            pltpu.VMEM((SEQ, SEQ), BF16),
            pltpu.VMEM((SEQ, SEQ), BF16),
            pltpu.VMEM(joint_shape, BF16),
            pltpu.VMEM((8, 128), F32),
            pltpu.VMEM((16, 2, CHUNK, width), BF16),
            pltpu.VMEM((7, 4, CHUNK, PADDED), BF16),
            pltpu.VMEM((4, CHUNK, PADDED), BF16),
            pltpu.VMEM((3, CHUNK, PADDED), BF16),
            pltpu.VMEM((16, CHUNK, width), BF16),
            pltpu.VMEM((16, CHUNK, width), BF16),
            pltpu.VMEM((3, 4, CHUNK, width), BF16),
            pltpu.VMEM((4, CHUNK, width), BF16),
            pltpu.VMEM((3, CHUNK, width), BF16),
            pltpu.VMEM((2, 8, 128), F32),
            pltpu.VMEM((2, 8, 128), F32),
            pltpu.VMEM((4, 8, 128), F32),
            pltpu.VMEM((4, 8, 128), F32),
            pltpu.VMEM((4, 8, 128), F32),
            pltpu.VMEM((4, 8, 128), F32),
            sem((2, 7, 4)),
            sem((2, 3)),
            sem((2, 4)),
            sem((2, 3)),
            sem((2, 3)),
            sem((2, 3)),
            sem((2, 7, 4)),
            sem((2, 2)),
            sem((2, 4, 3)),
        ],
        compiler_params=pltpu.CompilerParams(
            collective_id=0, has_side_effects=True, vmem_limit_bytes=58 * 2**20
        ),
    )(
        latent_with_rope.T,
        latent_norm_weight.reshape(1, LATENT),
        expand_weight,
        queries,
        grad_output,
    )
    grad_queries, joint_t, grad_up_weight, gain = pl.pallas_call(
        write_body,
        name="write",
        out_shape=(
            jax.ShapeDtypeStruct(queries.shape, BF16),
            jax.ShapeDtypeStruct((JOINT, SEQ), BF16),
            jax.ShapeDtypeStruct((CHUNK, width), F32),
            jax.ShapeDtypeStruct((1, LATENT), F32),
        ),
        in_specs=[hbm_spec()] * 4,
        out_specs=(hbm_spec(),) * 4,
        scratch_shapes=[
            pltpu.VMEM(queries.shape, BF16),
            pltpu.VMEM(joint_shape, BF16),
            pltpu.VMEM((CHUNK, width), F32),
            pltpu.VMEM((1, LATENT), F32),
            pltpu.VMEM((JOINT, SEQ), BF16),
            sem((8,)),
        ],
        compiler_params=pltpu.CompilerParams(vmem_limit_bytes=58 * 2**20),
    )(grad_query, joint, up, gain)
    return grad_queries, joint_t.T, grad_up_weight, gain.reshape(LATENT)


def solution(mesh):
    assert mesh.shape["dp"] == NX * NY * NCORE and mesh.shape["tensor"] == NZ * NLO
    placed = (P("dp", None), P(), P(None, "tensor"), P("dp", "tensor"), P("dp", "tensor"))
    return jax.shard_map(
        per_device,
        mesh=mesh,
        in_specs=placed,
        out_specs=(P("dp", "tensor"), P("dp", None), P("dp", "tensor"), P()),
        check_vma=False,
    )
```
